512 devices in a mesh: snap: 16 (over z), space: 32 (over x, y, core).
Axes of the slice: x: 4, y: 4, z: 16, core: 2. Of those that a mesh axis runs over, the one named last changes fastest.
Arguments:
- snapshots: bfloat16 [49152, 4096], P('space', 'snap'), may hold values from -6 to 6
- cell_volume: float32 [49152], P('space'), may hold values from 0.0004 to 32, as said below
- counts: int32 [32], P('space'), may hold values from 6 to 24, as said below
- rim_rows: int32 [32, 2], P('space'), may hold values from 0 to 23, as said below
- jac_cols: int32 [768, 8], P('space'), may hold values from 0 to 25, as said below
- jacobian: bfloat16 [49152, 512], P('space'), may hold values from -0.25 to 0.25
- omega: bfloat16 [2, 512, 256], replicated, may hold values from -0.25 to 0.25
Outputs:
- basis: bfloat16 [49152, 4096], P('space', 'snap')
- jac_basis: bfloat16 [49152, 4096], P('space', 'snap')
The draws below stay inside these ranges and needn't reach their ends.
Inputs may be any that keep to these rules, and one draw needn't show every extreme that they name: `counts`: some partition has exactly 24 used blocks. `rim_rows`: the 2 entries of a partition are distinct blocks below its count; entry 1 is its last used block. `jac_cols`: entry 0 of each block row is the block's own index; every other entry is below the partition's count or at least 24. `cell_volume`: Positive.
All inputs are finite; a program needn't handle non-finite values.
Results may differ from the reference program's by a relative error of at most 0.011.
Values may be sent and summed in bfloat16 or wider, within the bound.
A program may use at most 64 MiB of HBM per device.

```python
import jax
import jax.numpy as jnp
from jax import lax

BLOCK = 64
CAP = 24
R = 256
NNZ = 8
H = 1
LEVELS = 2
ROWS = 49152
S = 4096
N_SNAP = 16
N_SPACE = 32


def partition_counts(key):
    base = jax.random.fold_in(key, 101)
    first, second, third = jax.random.split(base, 3)
    span = CAP - CAP // 4
    lower = jnp.minimum(jax.random.randint(first, (N_SPACE,), 0, span + 1), jax.random.randint(second, (N_SPACE,), 0, span + 1))
    drawn = CAP // 4 + lower
    busiest = jax.random.randint(third, (), 0, N_SPACE)
    return jnp.where(jnp.arange(N_SPACE) == busiest, CAP, drawn).astype(jnp.int32)


def draw_counts(key, part):
    return partition_counts(key)


def draw_rim_rows(key, part):
    used = partition_counts(key)
    key = jax.random.fold_in(key, 2)
    noise = jax.random.randint(key, (N_SPACE, CAP), 0, 4096)
    order = lax.broadcasted_iota(jnp.int32, (N_SPACE, CAP), 1)
    limit = used[:, None] - H
    score = noise * CAP + order + jnp.where(order < limit, 0, 4096 * CAP + CAP)
    earlier = jnp.argsort(score, axis=1)[:, :H].astype(jnp.int32)
    later = limit + lax.broadcasted_iota(jnp.int32, (N_SPACE, H), 1)
    return jnp.concatenate([earlier, later], 1).astype(jnp.int32)


def draw_jac_cols(key, part):
    used = partition_counts(key)
    key = jax.random.fold_in(key, 3)
    local_count = jnp.repeat(used, CAP, total_repeat_length=N_SPACE * CAP)[:, None]
    limit = local_count + 2 * H
    raw = jax.random.randint(key, (N_SPACE * CAP, NNZ), 0, 1 << 30)
    pick = raw % limit
    mapped = jnp.where(pick < local_count, pick, CAP + pick - local_count)
    own = (jnp.arange(N_SPACE * CAP, dtype=jnp.int32) % CAP)[:, None]
    column = lax.broadcasted_iota(jnp.int32, (N_SPACE * CAP, NNZ), 1)
    return jnp.where(column == 0, own, mapped).astype(jnp.int32)


def draw_cell_volume(key, part):
    key = jax.random.fold_in(key, 7)
    first, second = jax.random.split(key)
    order = jax.random.permutation(first, N_SPACE).astype(jnp.float32)
    exponent = order / (N_SPACE - 1)
    region = 8.0 * jnp.exp(-exponent * jnp.log(4096.0))
    spread = jnp.repeat(region, CAP * BLOCK, total_repeat_length=N_SPACE * CAP * BLOCK)
    local = jnp.exp(jax.random.uniform(second, (N_SPACE * CAP * BLOCK,), jnp.float32, jnp.log(0.25), jnp.log(4.0)))
    return (spread * local).astype(jnp.float32)


def steps_of(key, dims, pieces, smallest, top_value):
    def one(dim, blocks):
        draws = jax.random.uniform(jax.random.fold_in(jax.random.fold_in(key, 6), dim), (blocks,), jnp.float32, smallest / len(pieces), top_value / len(pieces))
        return jnp.repeat(jnp.exp(draws), dims[dim] // blocks).reshape((-1,) + (1,) * (len(dims) - dim - 1))

    loudness = one(*pieces[0])
    for cut in pieces[1:]:
        loudness = loudness * one(*cut)
    return loudness


def centred(key, extent, deviation, most, shards=(), kind=jnp.bfloat16):
    result = deviation * jax.random.normal(key, extent, jnp.float32)
    if shards:
        result = result * steps_of(key, extent, shards, -0.22, 0.18)
    return jnp.clip(result, -most, most).astype(kind)


def setup_inputs(seed: int = 0) -> dict:
    streams_of = jax.random.split(jax.random.key(seed), 8)
    snapshots = centred(streams_of[0], (ROWS, S), 1.0, 6.0, ((0, 32), (1, 16)))
    cell_volume = draw_cell_volume(jax.random.fold_in(streams_of[7], 71), 0)
    counts = draw_counts(jax.random.fold_in(streams_of[7], 71), 0)
    rim_rows = draw_rim_rows(jax.random.fold_in(streams_of[7], 71), 0)
    jac_cols = draw_jac_cols(jax.random.fold_in(streams_of[7], 71), 0)
    jacobian = centred(streams_of[5], (ROWS, NNZ * BLOCK), (NNZ * BLOCK) ** -0.5, 0.25, ((0, 32),))
    omega = centred(streams_of[6], (LEVELS, 2 * R, R), (2 * R) ** -0.5, 0.25)
    return {"snapshots": snapshots, "cell_volume": cell_volume, "counts": counts, "rim_rows": rim_rows, "jac_cols": jac_cols, "jacobian": jacobian, "omega": omega}


HIGH = lax.Precision.HIGHEST

def inverse_factor(gram):
    factor = jnp.linalg.cholesky(gram)
    ident = jnp.eye(gram.shape[0], dtype=gram.dtype)
    return lax.linalg.triangular_solve(factor, ident, left_side=True, lower=True)

def orthonormal(columns, weight):
    gram = jnp.dot((columns * weight[:, None]).T, columns, precision=HIGH)
    return jnp.dot(columns, inverse_factor(gram).T, precision=HIGH).astype(jnp.bfloat16)

def take_rows(source, picks):
    return jnp.take(source, picks, axis=0)

def reference(snapshots, cell_volume, counts, rim_rows, jac_cols, jacobian, omega):
    total = snapshots.shape[0]
    index = jnp.arange(total, dtype=jnp.int32)
    block_index = index // BLOCK % CAP
    owner_count = jnp.repeat(counts, CAP * BLOCK, total_repeat_length=total)
    valid = (block_index < owner_count).astype(jnp.float32)
    weight = cell_volume * valid / total
    bases = []
    for batch in range(N_SNAP):
        local = snapshots[:, batch * R:(batch + 1) * R].astype(jnp.float32) * valid[:, None]
        bases.append(orthonormal(local, weight))
    for level in range(LEVELS):
        step = 1 << level
        merged = list(bases)
        for batch in range(N_SNAP):
            if batch & step:
                continue
            joined = jnp.concatenate([bases[batch], bases[batch + step]], 1)
            sketch = jnp.dot(joined.astype(jnp.float32), omega[level].astype(jnp.float32), preferred_element_type=jnp.float32)
            fresh = orthonormal(sketch, weight)
            merged[batch] = fresh
            merged[batch + step] = fresh
        bases = merged
    group = 1 << LEVELS
    cols = jac_cols.reshape(N_SPACE, CAP, NNZ)
    blocks_jac = jacobian.reshape(N_SPACE, CAP, BLOCK, NNZ, BLOCK)
    valid_rows = valid[:, None]
    basis_parts = []
    product_parts = []
    for leader in range(0, N_SNAP, group):
        rounded = bases[leader]
        blocked = rounded.reshape(N_SPACE, CAP, BLOCK, R)
        rims = jax.vmap(take_rows)(blocked, rim_rows)
        zero = jnp.zeros((1, H, BLOCK, R), jnp.bfloat16)
        from_prev = jnp.concatenate([zero, rims[:-1, H:]], 0)
        from_next = jnp.concatenate([rims[1:, :H], zero], 0)
        extended = jnp.concatenate([blocked, from_prev, from_next], 1)
        total_sum = jnp.zeros((N_SPACE, CAP, BLOCK, R), jnp.float32)
        for slot in range(NNZ):
            picked = jax.vmap(take_rows)(extended, cols[:, :, slot]).astype(jnp.float32)
            matrix = blocks_jac[:, :, :, slot, :].astype(jnp.float32)
            total_sum = total_sum + jnp.einsum('pcij,pcjr->pcir', matrix, picked, precision=HIGH)
        product = (total_sum.reshape(total, R) * valid_rows).astype(jnp.bfloat16)
        for member in range(group):
            basis_parts.append(rounded)
            product_parts.append(product)
    return (jnp.concatenate(basis_parts, 1), jnp.concatenate(product_parts, 1))
```

```python
import functools

import jax
import jax.numpy as jnp
from jax import lax
from jax.experimental import pallas as pl
from jax.experimental.pallas import tpu as pltpu
from jax.sharding import PartitionSpec as P

BLOCK = 64
NNZ = 8
LEVELS = 2
F32, BF16 = jnp.float32, jnp.bfloat16
NN = ((1,), (0,))
NT = ((1,), (1,))
TN = ((0,), (0,))
MESH = pl.DeviceIdType.MESH
VMEM_LIMIT = 48 * 1024 * 1024


def split(a):
    hi = a.astype(BF16)
    return hi, (a - hi.astype(F32)).astype(BF16)

def mm(a, b, dims=((1,), (0,))):
    return lax.dot_general(a, b, (dims, ((), ())), preferred_element_type=F32)


def mm3(a, b, dims=NN):
    ah, al = split(a)
    bh, bl = split(b)
    return mm(ah, bh, dims) + (mm(ah, bl, dims) + mm(al, bh, dims))

def leaf(aq, W=32):
    T = W // 8
    def panel(k, _):
        r0 = pl.multiple_of(k * W, W)
        rows = aq[pl.ds(r0, W), :]
        diag = pltpu.roll(rows[:, :128], lax.rem(128 - r0, 128), axis=1)
        C = [[jnp.broadcast_to(diag[8*t:8*t+8, m:m+1], (8, 128)) for t in range(T)] for m in range(W)]
        lane = lax.broadcasted_iota(jnp.int32, (8, 128), 1)
        sub = lax.broadcasted_iota(jnp.int32, (8, 128), 0)
        E = [(lane == sub + 8*t).astype(F32) for t in range(T)]
        scale = [jnp.zeros((8, 128), F32) for t in range(T)]
        for j in range(W):
            tj, sj = divmod(j, 8)
            piv = jnp.broadcast_to(C[j][tj][sj:sj+1, :], (8, 128))
            r = pl.reciprocal(piv, approx=True)
            r = r * (2.0 - piv * r)
            f = [None]*T
            for t in range(tj, T):
                f[t] = C[j][t] * r
            f[tj] = jnp.where(sub > sj, f[tj], 0.0)
            for m in range(j + 1, W):
                tm, sm = divmod(m, 8)
                c = jnp.broadcast_to(C[j][tm][sm:sm+1, :], (8, 128))
                for t in range(tm, T):
                    C[m][t] = C[m][t] - f[t] * c
            e = jnp.broadcast_to(E[tj][sj:sj+1, :], (8, 128))
            for t in range(tj, T):
                E[t] = E[t] - f[t] * e
            scale[tj] = jnp.where(sub == sj, piv, scale[tj])
        E = [E[t] * lax.rsqrt(scale[t]) for t in range(T)]
        inv = jnp.concatenate(E, 0)[:, :W]
        R = mm3(inv, rows)
        low = jnp.transpose(R[:, :128])
        low = jnp.where(lax.broadcasted_iota(jnp.int32, low.shape, 0) >= r0 + W, low, 0.0)
        aq[...] = aq[...] - mm3(low, R)
        aq[pl.ds(r0, W), :] = R
        return 0
    lax.fori_loop(0, 128 // W, panel, 0)

def chol_inv(a, z, aq, W=32):
    eye = (lax.broadcasted_iota(jnp.int32, (128, 128), 0) == lax.broadcasted_iota(jnp.int32, (128, 128), 1)).astype(F32)
    aq[:, 128:] = eye
    aq[:, :128] = a[:128, :128]
    leaf(aq, W)
    z11 = aq[:, 128:]
    z[:128, :128] = z11
    l21 = mm3(a[128:, :128], z11, NT)
    aq[:, :128] = a[128:, 128:] - mm3(l21, l21, NT)
    aq[:, 128:] = eye
    m21 = mm3(l21, z11)
    leaf(aq, W)
    z22 = aq[:, 128:]
    z[128:, 128:] = z22
    z[128:, :128] = -mm3(z22, m21)
    z[:128, 128:] = jnp.zeros((128, 128), F32)


def reduce_gram(a_ref, b_ref, w_ref, out_ref, part, arrived, total, gathered, sems):
    n = part.shape[0]
    me = lax.axis_index("space")
    barrier = pltpu.get_barrier_semaphore()

    def greet(t, _):
        peer = lax.rem(me + t, n)
        pl.semaphore_signal(barrier, inc=1, device_id={"space": peer}, device_id_type=MESH)
        return 0

    lax.fori_loop(1, n, greet, 0)
    weighted = jnp.transpose(a_ref[...]).astype(F32) * w_ref[...]
    high, low = split(weighted)
    gram = mm(high, b_ref[...]) + mm(low, b_ref[...])
    part[...] = gram.reshape(part.shape)
    pl.semaphore_wait(barrier, n - 1)

    def scatter(t, _):
        peer = lax.rem(me + t, n)
        pltpu.make_async_remote_copy(
            src_ref=part.at[peer],
            dst_ref=arrived.at[me],
            send_sem=sems.at[0],
            recv_sem=sems.at[1],
            device_id={"space": peer},
            device_id_type=MESH,
        ).start()
        return 0

    lax.fori_loop(1, n, scatter, 0)
    arrived[me] = part[me]
    whole = arrived.at[pl.ds(0, n - 1)]
    pltpu.make_async_copy(whole, whole, sems.at[1]).wait()
    total[...] = jnp.sum(arrived[...], axis=0)

    def gather(t, _):
        peer = lax.rem(me + t, n)
        pltpu.make_async_remote_copy(
            src_ref=total,
            dst_ref=gathered.at[me],
            send_sem=sems.at[2],
            recv_sem=sems.at[3],
            device_id={"space": peer},
            device_id_type=MESH,
        ).start()
        return 0

    lax.fori_loop(1, n, gather, 0)
    gathered[me] = total[...]
    pltpu.make_async_copy(whole, whole, sems.at[0]).wait()
    other = gathered.at[pl.ds(0, n - 1)]
    pltpu.make_async_copy(other, other, sems.at[2]).wait()
    pltpu.make_async_copy(other, other, sems.at[3]).wait()
    out_ref[...] = gathered[...].reshape(out_ref.shape)


def space_gram(a, b, weight):
    n = lax.axis_size("space")
    rank = a.shape[1]
    chunk = (n, rank // n, rank)
    return pl.pallas_call(
        reduce_gram,
        out_shape=jax.ShapeDtypeStruct((rank, rank), F32),
        in_specs=[pl.BlockSpec(memory_space=pltpu.VMEM)] * 3,
        out_specs=pl.BlockSpec(memory_space=pltpu.VMEM),
        scratch_shapes=[
            pltpu.VMEM(chunk, F32),
            pltpu.VMEM(chunk, F32),
            pltpu.VMEM(chunk[1:], F32),
            pltpu.VMEM(chunk, F32),
            pltpu.SemaphoreType.DMA((4,)),
        ],
        compiler_params=pltpu.CompilerParams(
            collective_id=0, has_side_effects=True, vmem_limit_bytes=VMEM_LIMIT
        ),
        name="space_gram",
    )(a, b, weight)


def first_kernel(x_ref, g_ref, out_ref, z, aq):
    chol_inv(g_ref, z, aq)
    high, low = split(z[...])
    out_ref[...] = (mm(x_ref[...], high, NT) + mm(x_ref[...], low, NT)).astype(BF16)


def merge_kernel(lo_ref, hi_ref, b_ref, om_ref, out_ref, m, z, aq):
    rank = b_ref.shape[0]
    oa, ob = om_ref[:rank, :], om_ref[rank:, :]
    bh, bl = split(b_ref[...])
    cross = mm3(jnp.transpose(oa).astype(F32), mm(bh, ob) + mm(bl, ob))
    z[...] = cross
    m[...] = mm(om_ref[...], om_ref[...], TN)
    m[...] = m[...] + z[...] + jnp.transpose(z[...])
    chol_inv(m, z, aq)
    sketch = mm(lo_ref[...], oa) + mm(hi_ref[...], ob)
    out_ref[...] = mm3(sketch, z[...], NT).astype(BF16)


def local_call(body, shape, scratch, name):
    return pl.pallas_call(
        body,
        out_shape=jax.ShapeDtypeStruct(shape, BF16),
        scratch_shapes=scratch,
        compiler_params=pltpu.CompilerParams(vmem_limit_bytes=VMEM_LIMIT),
        name=name,
    )


def shifted(block, axis, distance):
    devices = range(lax.axis_size(axis))
    route = [(i - distance, i) for i in devices if i - distance in devices]
    return lax.ppermute(block, axis, route)


def on_device(snapshots, cell_volume, counts, rim_rows, jac_cols, jacobian, omega):
    rows, rank = snapshots.shape
    blocks = rows // BLOCK
    total = rows * lax.axis_size("space")
    block_index = lax.broadcasted_iota(jnp.int32, (blocks, BLOCK), 0).reshape(rows)
    valid = block_index < counts[0]
    weight = jnp.where(valid, cell_volume / total, 0.0).reshape(1, rows)
    local = jnp.where(valid[:, None], snapshots, 0)
    square = pltpu.VMEM((rank, rank), F32)
    wide = pltpu.VMEM((rank // 2, rank), F32)
    gram = space_gram(local, local, weight)
    current = local_call(first_kernel, (rows, rank), [square, wide], "orthonormal")(local, gram)
    position = lax.axis_index("snap")
    for level in range(LEVELS):
        step = 1 << level
        partner = [(i, i ^ step) for i in range(lax.axis_size("snap"))]
        incoming = lax.ppermute(current, "snap", partner)
        upper = position // step % 2 == 1
        lower_base = jnp.where(upper, incoming, current)
        higher_base = jnp.where(upper, current, incoming)
        cross = space_gram(lower_base, higher_base, weight)
        current = local_call(merge_kernel, (rows, rank), [square, square, wide], "merge")(
            lower_base, higher_base, cross, omega[level]
        )
    blocked = current.reshape(blocks, BLOCK, rank)
    rims = jnp.take(blocked, rim_rows[0], axis=0)
    before = shifted(rims[1], "space", 1)
    after = shifted(rims[0], "space", -1)
    extended = jnp.concatenate([blocked, before[None], after[None]], 0)
    picked = jnp.take(extended, jac_cols, axis=0)
    matrix = jacobian.reshape(blocks, BLOCK, NNZ, BLOCK)
    product = jnp.einsum("bikj,bkjr->bir", matrix, picked, preferred_element_type=F32)
    product = jnp.where(valid[:, None], product.reshape(rows, rank), 0.0)
    return (current, product.astype(BF16))


def solution(mesh):
    in_specs = (
        P("space", "snap"),
        P("space"),
        P("space"),
        P("space", None),
        P("space", None),
        P("space", None),
        P(),
    )
    out_specs = (P("space", "snap"), P("space", "snap"))
    return jax.shard_map(
        on_device, mesh=mesh, in_specs=in_specs, out_specs=out_specs, check_vma=False
    )
```

```python
import functools

import jax
import jax.numpy as jnp
from jax import lax
from jax.experimental import pallas as pl
from jax.experimental.pallas import tpu as pltpu
from jax.sharding import PartitionSpec as P

BLOCK = 64
NNZ = 8
LEVELS = 2
F32, BF16 = jnp.float32, jnp.bfloat16
NN = ((1,), (0,))
NT = ((1,), (1,))
TN = ((0,), (0,))
MESH = pl.DeviceIdType.MESH
VMEM_LIMIT = 48 * 1024 * 1024


def split(a):
    hi = a.astype(BF16)
    return hi, (a - hi.astype(F32)).astype(BF16)

def mm(a, b, dims=((1,), (0,))):
    return lax.dot_general(a, b, (dims, ((), ())), preferred_element_type=F32)


def mm3(a, b, dims=NN):
    ah, al = split(a)
    bh, bl = split(b)
    return mm(ah, bh, dims) + (mm(ah, bl, dims) + mm(al, bh, dims))

def leaf(aq, W=32):
    T = W // 8
    def panel(k, _):
        r0 = pl.multiple_of(k * W, W)
        rows = aq[pl.ds(r0, W), :]
        diag = pltpu.roll(rows[:, :128], lax.rem(128 - r0, 128), axis=1)
        C = [[jnp.broadcast_to(diag[8*t:8*t+8, m:m+1], (8, 128)) for t in range(T)] for m in range(W)]
        lane = lax.broadcasted_iota(jnp.int32, (8, 128), 1)
        sub = lax.broadcasted_iota(jnp.int32, (8, 128), 0)
        E = [(lane == sub + 8*t).astype(F32) for t in range(T)]
        scale = [jnp.zeros((8, 128), F32) for t in range(T)]
        for j in range(W):
            tj, sj = divmod(j, 8)
            piv = jnp.broadcast_to(C[j][tj][sj:sj+1, :], (8, 128))
            r = pl.reciprocal(piv, approx=True)
            f = [None]*T
            for t in range(tj, T):
                f[t] = C[j][t] * r
            f[tj] = jnp.where(sub > sj, f[tj], 0.0)
            for m in range(j + 1, W):
                tm, sm = divmod(m, 8)
                c = jnp.broadcast_to(C[j][tm][sm:sm+1, :], (8, 128))
                for t in range(tm, T):
                    C[m][t] = C[m][t] - f[t] * c
            e = jnp.broadcast_to(E[tj][sj:sj+1, :], (8, 128))
            for t in range(tj, T):
                E[t] = E[t] - f[t] * e
            scale[tj] = jnp.where(sub == sj, piv, scale[tj])
        E = [E[t] * lax.rsqrt(scale[t]) for t in range(T)]
        inv = jnp.concatenate(E, 0)[:, :W]
        R = mm3(inv, rows)
        low = jnp.transpose(R[:, :128])
        low = jnp.where(lax.broadcasted_iota(jnp.int32, low.shape, 0) >= r0 + W, low, 0.0)
        aq[...] = aq[...] - mm3(low, R)
        aq[pl.ds(r0, W), :] = R
        return 0
    lax.fori_loop(0, 128 // W, panel, 0)

def chol_upper(a, z, aq):
    ident = eye(128)
    aq[:, 128:] = ident
    aq[:, :128] = a[:128, :128]
    leaf(aq)
    z11 = aq[:, 128:]
    z[:128, :128] = z11
    l21 = mm3(a[128:, :128], z11, NT)
    aq[:, :128] = a[128:, 128:] - mm3(l21, l21, NT)
    aq[:, 128:] = ident
    z[128:, :128] = mm3(l21, z11)


def chol_lower(z, aq):
    leaf(aq)
    z22 = aq[:, 128:]
    z[128:, 128:] = z22
    z[128:, :128] = -mm3(z22, z[128:, :128])
    z[:128, 128:] = jnp.zeros((128, 128), F32)


def chol_inv(a, z, aq):
    chol_upper(a, z, aq)
    chol_lower(z, aq)


def iota(shape, dim):
    return lax.broadcasted_iota(jnp.int32, shape, dim)


def eye(n):
    return (iota((n, n), 0) == iota((n, n), 1)).astype(F32)


def mm3s(a, b, dims=NN):
    return mm(a[0], b[0], dims) + (mm(a[0], b[1], dims) + mm(a[1], b[0], dims))


def mm2(a, b, dims=NN):
    high, low = split(a)
    return mm(high, b, dims) + mm(low, b, dims)


def mm2r(a, b, dims=NN):
    high, low = split(b)
    return mm(a, high, dims) + mm(a, low, dims)


def newton_step(a_ref, z_ref):
    a = a_ref[...]
    row, col = iota(a.shape, 0), iota(a.shape, 1)
    h = split(jnp.where(row > col, -a, jnp.where(row == col, 1.5 - 0.5 * a, 0.0)))
    t = mm3s(h, split(a))
    z = mm3s(h, split(z_ref[...]))
    a_ref[...] = mm3s(split(t), h, NT)
    z_ref[...] = z


def residual(a, count):
    worst = jnp.float32(0.0)
    for i in range(count):
        off = a[i] - eye(a.shape[1])
        total = jnp.sum(off * off)
        worst = jnp.maximum(worst, jnp.where(total < 1e30, total, 1e30))
    return worst


def factor(a, z, first, start, wide, count, fixed, most):
    for i in range(count):
        first[i] = a[i]
        start[i] = z[i]
    for _ in range(fixed):
        for i in range(count):
            newton_step(a.at[i], z.at[i])

    def unsettled(state):
        return jnp.logical_and(state[0] < most, state[1] > 1e-7)

    def again(state):
        for i in range(count):
            newton_step(a.at[i], z.at[i])
        return state[0] + 1, residual(a, count)

    left = lax.while_loop(unsettled, again, (jnp.int32(fixed), residual(a, count)))[1]

    @pl.when(left > 1e-7)
    def _():
        def direct(i, _):
            chol_inv(first.at[i], z.at[i], wide)
            z[i] = mm3(z[i], start[i])
            return 0

        lax.fori_loop(0, count, direct, 0)


class Phases:
    def __init__(self, sends, arrivals):
        self.sends, self.arrivals = sends, arrivals
        self.flying = []
        me = lax.axis_index("space")
        self.core = lax.rem(me, 2)
        self.y = lax.rem(me // 2, 4)
        self.x = me // 8
        self.snap = lax.axis_index("snap")
        self.place = lax.rem(self.snap, 4)
        self.used = 0

    def space(self, x, y, core):
        return (x * 4 + y) * 2 + core

    def peers(self):
        found = [{"space": self.space(self.x, self.y, 1 - self.core)}]
        for d in (1, 2, 3):
            found.append({"space": self.space(lax.rem(self.x + d, 4), self.y, self.core)})
            found.append({"space": self.space(self.x, lax.rem(self.y + d, 4), self.core)})
            found.append({"snap": self.other(d)})
        return found

    def other(self, d):
        place = self.place
        if d & 1:
            place = place + 1 - 2 * lax.rem(place, 2)
        if d & 2:
            place = place + 2 - 4 * (place // 2)
        return self.snap - self.place + place

    def send(self, src, dst, device):
        slot = self.used
        self.used += 1
        copy = pltpu.make_async_remote_copy(
            src_ref=src,
            dst_ref=dst,
            send_sem=self.sends.at[slot],
            recv_sem=self.arrivals.at[slot],
            device_id=device,
            device_id_type=MESH,
        )
        copy.start()
        self.flying.append(copy)
        return copy

    def finish(self):
        for copy in self.flying:
            copy.wait_send()

    def greet(self, devices):
        barrier = pltpu.get_barrier_semaphore()
        for device in devices:
            pl.semaphore_signal(barrier, inc=1, device_id=device, device_id_type=MESH)

    def met(self, count):
        pl.semaphore_wait(pltpu.get_barrier_semaphore(), count)

    def along(self, half, major, d):
        if (half == 0) == major:
            place = lax.rem(self.x + d, 4)
            return place, {"space": self.space(place, self.y, self.core)}
        place = lax.rem(self.y + d, 4)
        return place, {"space": self.space(self.x, place, self.core)}

    def own(self, half, major):
        return self.x if (half == 0) == major else self.y


def rows_of(place, size):
    return pl.ds(pl.multiple_of(place * size, size), size)


def sum_over_space(ph, part, bc, bx, by, s1, s2, s3, spread, beside=None):
    copy = ph.send(
        part.at[:, :, rows_of(1 - ph.core, 128), :],
        bc,
        {"space": ph.space(ph.x, ph.y, 1 - ph.core)},
    )
    copy.wait_recv()
    s1[...] = part[:, :, rows_of(ph.core, 128), :] + bc[...]
    copies = []
    for d in (1, 2, 3):
        for half in (0, 1):
            place, device = ph.along(half, True, d)
            copies.append(ph.send(s1.at[half, :, rows_of(place, 32), :], bx.at[half, d - 1], device))
    if beside is not None:
        beside()
    for copy in copies:
        copy.wait_recv()
    for half in (0, 1):
        mine = s1[half, :, rows_of(ph.own(half, True), 32), :]
        s2[half] = mine + (bx[half, 0] + bx[half, 1] + bx[half, 2])
    copies = []
    for d in (1, 2, 3):
        for half in (0, 1):
            place, device = ph.along(half, False, d)
            copies.append(ph.send(s2.at[half, :, rows_of(place, 8), :], by.at[half, d - 1], device))
    for copy in copies:
        copy.wait_recv()
    for half in (0, 1):
        mine = s2[half, :, rows_of(ph.own(half, False), 8), :]
        s3[half] = mine + (by[half, 0] + by[half, 1] + by[half, 2])
    copies = []
    for d in (1, 2, 3):
        copies.append(ph.send(s3, spread.at[d], {"snap": ph.other(d)}))
    spread[0] = s3[...]
    for copy in copies:
        copy.wait_recv()


def give_over_space(ph, chunk, g1, g2, out):
    copies = []
    for half in (0, 1):
        mine = rows_of(ph.own(half, False), 8)
        for d in (1, 2, 3):
            _, device = ph.along(half, False, d)
            copies.append(ph.send(chunk.at[half], g1.at[half, :, mine, :], device))
        g1[half, :, mine, :] = chunk[half]
    for copy in copies:
        copy.wait_recv()
    copies = []
    for half in (0, 1):
        mine = rows_of(ph.own(half, True), 32)
        for d in (1, 2, 3):
            _, device = ph.along(half, True, d)
            copies.append(ph.send(g1.at[half], g2.at[half, :, mine, :], device))
        g2[half, :, mine, :] = g1[half]
    for copy in copies:
        copy.wait_recv()
    mine = rows_of(ph.core, 128)
    copy = ph.send(
        g2, out.at[:, :, mine, :], {"space": ph.space(ph.x, ph.y, 1 - ph.core)}
    )
    out[:, :, mine, :] = g2[...]
    copy.wait_recv()


def put_halves(ref, index, square):
    ref[0, index] = square[:, :128]
    ref[1, index] = square[:, 128:]


def whole(ref, index):
    return jnp.concatenate([ref[0, index], ref[1, index]], axis=1)


def quarter_rows(place, size):
    return rows_of(2 * lax.rem(place, 2) + place // 2, size)


def first_sum(
    x_ref, w_ref, om_ref, out_ref, parts_ref, zo_ref,
    part, bc, bx, by, s1, s2, s3, spread, chunk, g1, g2, got, sends, arrivals, parts, m, zo, wide
):
    ph = Phases(sends, arrivals)
    ph.greet(ph.peers())
    weighted = jnp.transpose(x_ref[...]).astype(F32) * w_ref[...]
    put_halves(part, 0, mm2(weighted, x_ref[...]))
    ph.met(10)
    quarter = parts.shape[1]

    def give_rows(d):
        there = ph.other(d)
        rows = quarter_rows(lax.rem(there, 4), quarter)
        return ph.send(x_ref.at[rows, :], parts.at[d - 1], {"snap": there})

    bulk = [give_rows(2), give_rows(1)]
    om = om_ref[ph.core]
    m[...] = mm(om, om, TN)
    mine = zo.at[ph.core]
    sum_over_space(
        ph, part, bc, bx, by, s1, s2, s3, spread, lambda: chol_upper(m, mine, wide)
    )
    bulk.append(give_rows(3))
    for d in range(4):
        chunk[:, d] = spread[d, :, 0]
    give_over_space(ph, chunk, g1, g2, got)
    chol_lower(mine, wide)
    factor_copy = ph.send(mine, mine, {"space": ph.space(ph.x, ph.y, 1 - ph.core)})
    for d in range(4):
        out_ref[d] = whole(got, d)
    for copy in bulk:
        copy.wait_recv()
    parts_ref[...] = parts[...]
    factor_copy.wait_recv()
    zo_ref[...] = zo[...]
    ph.finish()


def second_sum(part, out_ref, bc, bx, by, s1, s2, s3, spread, chunk, g1, g2, got, sends, arrivals):
    ph = Phases(sends, arrivals)
    ph.greet(ph.peers())
    ph.met(10)
    sum_over_space(ph, part, bc, bx, by, s1, s2, s3, spread)
    chunk[...] = (spread[0] + spread[1]) + (spread[2] + spread[3])
    give_over_space(ph, chunk, g1, g2, got)
    for d in range(3):
        out_ref[d] = whole(got, d)
    ph.finish()


def sum_scratch(before, after, copies=29):
    return [
        pltpu.VMEM((2, before, 128, 128), F32),
        pltpu.VMEM((2, 3, before, 32, 128), F32),
        pltpu.VMEM((2, 3, before, 8, 128), F32),
        pltpu.VMEM((2, before, 128, 128), F32),
        pltpu.VMEM((2, before, 32, 128), F32),
        pltpu.VMEM((2, before, 8, 128), F32),
        pltpu.VMEM((4, 2, before, 8, 128), F32),
        pltpu.VMEM((2, after, 8, 128), F32),
        pltpu.VMEM((2, after, 32, 128), F32),
        pltpu.VMEM((2, after, 128, 128), F32),
        pltpu.VMEM((2, after, 256, 128), F32),
        pltpu.SemaphoreType.DMA((copies,)),
        pltpu.SemaphoreType.DMA((copies,)),
    ]


def basis_kernel(place_ref, g_ref, x0, xs, w_ref, om_ref, sk_ref, part_ref, a, z, first, start, wide, base):
    place = place_ref[0]
    rank = om_ref.shape[2]
    diagonal = iota((rank, rank), 0) == iota((rank, rank), 1)
    for d in range(4):
        g = g_ref[d]
        pivots = jnp.where(diagonal, g, 0.0)
        down = lax.rsqrt(jnp.sum(pivots, axis=1, keepdims=True))
        across = lax.rsqrt(jnp.sum(pivots, axis=0, keepdims=True))
        a[d] = g * down * across
        z[d] = jnp.where(diagonal, down, 0.0)
    factor(a, z, first, start, wide, 4, 3, 8)
    for d in range(4):
        x = x0[...] if d == 0 else xs[d - 1]
        base[place ^ d] = mm2r(x, z[d], NT).astype(BF16)
    weight = w_ref[...]
    for pair in (0, 1):
        low, high = base[2 * pair], base[2 * pair + 1]
        sketch = mm(low, om_ref[0, :rank, :]) + mm(high, om_ref[0, rank:, :])
        sk_ref[:, pair * rank : (pair + 1) * rank] = sketch.astype(BF16)
        put_halves(part_ref, pair, mm2(jnp.transpose(low).astype(F32) * weight, high))
    low, high = sk_ref[:, :rank], sk_ref[:, rank:]
    put_halves(part_ref, 2, mm2(jnp.transpose(low).astype(F32) * weight, high))


def near_identity(z, om, cross, a, t):
    rank = cross.shape[0]
    qa = mm2(z, om[:rank], NT)
    qb = mm2r(om[rank:], z, NT)
    t[...] = mm3(qa, mm3(cross, qb))
    a[...] = eye(rank) + t[...] + jnp.transpose(t[...])


def final_kernel(c_ref, om_ref, zo_ref, sk_ref, out_ref, a, z, first, start, t, wide):
    rank = om_ref.shape[2]
    for pair in (0, 1):
        near_identity(zo_ref[0], om_ref[0], c_ref[pair], a.at[pair], t.at[pair])
        z[pair] = zo_ref[0]
    factor(a, z, first, start, wide, 2, 3, 8)
    cross = mm3(mm3(z[0], c_ref[2]), z[1], NT)
    near_identity(zo_ref[1], om_ref[1], cross, a.at[2], t.at[0])
    z[2] = zo_ref[1]
    factor(
        a.at[pl.ds(2, 1)], z.at[pl.ds(2, 1)], first, start, wide, 1, 3, 8
    )
    last = z[2]
    for pair in (0, 1):
        u = mm2r(om_ref[1, pair * rank : (pair + 1) * rank, :], last, NT)
        t[pair] = mm3(jnp.transpose(z[pair]), u)
    left, right = split(t[0]), split(t[1])
    low, high = sk_ref[:, :rank], sk_ref[:, rank:]
    final = (mm(low, left[0]) + mm(high, right[0])) + (mm(low, left[1]) + mm(high, right[1]))
    out_ref[...] = final.astype(BF16)


def spread_kernel(rim_ref, own_ref, base_ref, rims_ref, base, rim_out, rim_in, sends, arrivals):
    ph = Phases(sends, arrivals)
    near, far = ph.other(1), ph.other(2)
    me, n = lax.axis_index("space"), lax.axis_size("space")
    before, after = {"space": lax.rem(me + n - 1, n)}, {"space": lax.rem(me + 1, n)}
    ph.greet([{"snap": near}, {"snap": far}, before, after])
    quarter = own_ref.shape[0] // BLOCK
    pieces = 3
    size = quarter // pieces

    def rows(place, piece):
        return pl.ds((2 * lax.rem(place, 2) + place // 2) * quarter + piece * size, size)

    own = own_ref[...].reshape(quarter, BLOCK, own_ref.shape[1])
    for piece in range(pieces):
        base[rows(ph.place, piece)] = own[piece * size : (piece + 1) * size]
    ph.met(4)
    across, relayed = [], []
    for piece in range(pieces):
        mine = base.at[rows(ph.place, piece)]
        across.append(ph.send(mine, mine, {"snap": far}))
    for piece in range(pieces):
        mine = base.at[rows(ph.place, piece)]
        relayed.append(ph.send(mine, mine, {"snap": near}))
    for piece in range(pieces):
        across[piece].wait_recv()
        theirs = base.at[rows(lax.rem(far, 4), piece)]
        relayed.append(ph.send(theirs, theirs, {"snap": near}))
    for copy in relayed:
        copy.wait_recv()
    for side in (0, 1):
        rim_out[side] = base[rim_ref[0, side]]

    swaps = [
        ph.send(rim_out.at[0], rim_in.at[1], before),
        ph.send(rim_out.at[1], rim_in.at[0], after),
    ]
    base_ref[...] = base[...].reshape(base_ref.shape)
    for copy in swaps:
        copy.wait_recv()
    rims_ref[:BLOCK, :] = jnp.where(me > 0, rim_in[0], 0)
    rims_ref[BLOCK:, :] = jnp.where(me < n - 1, rim_in[1], 0)
    ph.finish()


def product_kernel(cols_ref, count_ref, full_ref, rims_ref, jac_ref, base_ref, out_ref, held):
    rows, rank = full_ref.shape
    blocks = rows // BLOCK
    base_ref[...] = full_ref[...]
    held[:rows, :] = full_ref[...]
    held[rows:, :] = rims_ref[...]
    count = count_ref[0]

    def block(b, _):
        here = pl.ds(pl.multiple_of(b * BLOCK, BLOCK), BLOCK)
        picked = [
            held[pl.ds(pl.multiple_of(cols_ref[b, k] * BLOCK, BLOCK), BLOCK), :] for k in range(NNZ)
        ]
        product = mm(jac_ref[here, :], jnp.concatenate(picked, axis=0))
        out_ref[here, :] = jnp.where(b < count, product, 0.0).astype(BF16)
        return 0

    lax.fori_loop(0, blocks, block, 0, unroll=2)


VM = pl.BlockSpec(memory_space=pltpu.VMEM)
SM = pl.BlockSpec(memory_space=pltpu.SMEM)


def call(body, outs, ins, scratch, name, **params):
    return pl.pallas_call(
        body,
        out_shape=outs,
        in_specs=ins,
        out_specs=jax.tree.map(lambda _: VM, outs),
        scratch_shapes=scratch,
        compiler_params=pltpu.CompilerParams(vmem_limit_bytes=VMEM_LIMIT, **params),
        name=name,
    )


def on_device(snapshots, cell_volume, counts, rim_rows, jac_cols, jacobian, omega):
    rows, rank = snapshots.shape
    blocks, quarter = rows // BLOCK, rows // 4
    total = rows * lax.axis_size("space")
    valid = lax.broadcasted_iota(jnp.int32, (blocks, BLOCK), 0).reshape(rows) < counts[0]
    weight = jnp.where(valid, cell_volume / total, 0.0).reshape(1, rows)
    local = jnp.where(valid[:, None], snapshots, 0)
    place = lax.axis_index("snap") % 4
    start = (2 * (place % 2) + place // 2) * quarter
    square = (rank, rank)
    wide = pltpu.VMEM((rank // 2, rank), F32)

    def squares(n):
        return pltpu.VMEM((n, rank, rank), F32)

    grams, others, starts = call(
        first_sum,
        [
            jax.ShapeDtypeStruct((4, rank, rank), F32),
            jax.ShapeDtypeStruct((3, quarter, rank), BF16),
            jax.ShapeDtypeStruct((2, rank, rank), F32),
        ],
        [VM] * 3,
        [pltpu.VMEM((2, 1, rank, rank // 2), F32)]
        + sum_scratch(1, 4, 33)
        + [pltpu.VMEM((3, quarter, rank), BF16), pltpu.VMEM(square, F32), squares(2), wide],
        "first_sum",
        collective_id=0,
        has_side_effects=True,
    )(local, weight, omega)
    sketch, cross = call(
        basis_kernel,
        [
            jax.ShapeDtypeStruct((quarter, 2 * rank), BF16),
            jax.ShapeDtypeStruct((2, 3, rank, rank // 2), F32),
        ],
        [SM] + [VM] * 5,
        [squares(4)] * 4 + [wide, pltpu.VMEM((4, quarter, rank), BF16)],
        "bases",
    )(
        place.reshape(1),
        grams,
        lax.dynamic_slice_in_dim(local, start, quarter, 0),
        others,
        lax.dynamic_slice_in_dim(weight, start, quarter, 1),
        omega,
    )
    cross = call(
        second_sum,
        jax.ShapeDtypeStruct((3, rank, rank), F32),
        [VM],
        sum_scratch(3, 3),
        "second_sum",
        collective_id=1,
        has_side_effects=True,
    )(cross)
    final = call(
        final_kernel,
        jax.ShapeDtypeStruct((quarter, rank), BF16),
        [VM] * 4,
        [squares(3), squares(3), squares(2), squares(2), squares(2), wide],
        "final_rows",
    )(cross, omega, starts, sketch)
    full, rims = call(
        spread_kernel,
        [
            jax.ShapeDtypeStruct((rows, rank), BF16),
            jax.ShapeDtypeStruct((2 * BLOCK, rank), BF16),
        ],
        [SM, VM],
        [
            pltpu.VMEM((blocks, BLOCK, rank), BF16),
            pltpu.VMEM((2, BLOCK, rank), BF16),
            pltpu.VMEM((2, BLOCK, rank), BF16),
            pltpu.SemaphoreType.DMA((11,)),
            pltpu.SemaphoreType.DMA((11,)),
        ],
        "spread_rows",
        collective_id=2,
        has_side_effects=True,
    )(rim_rows, final)
    basis, product = call(
        product_kernel,
        [jax.ShapeDtypeStruct((rows, rank), BF16)] * 2,
        [SM, SM, VM, VM, VM],
        [pltpu.VMEM((rows + 2 * BLOCK, rank), BF16)],
        "jac_product",
    )(jac_cols, counts, full, rims, jacobian)
    return (basis, product)


def solution(mesh):
    in_specs = (
        P("space", "snap"),
        P("space"),
        P("space"),
        P("space", None),
        P("space", None),
        P("space", None),
        P(),
    )
    out_specs = (P("space", "snap"), P("space", "snap"))
    return jax.shard_map(
        on_device, mesh=mesh, in_specs=in_specs, out_specs=out_specs, check_vma=False
    )
```

```python
import functools

import jax
import jax.numpy as jnp
from jax import lax
from jax.experimental import pallas as pl
from jax.experimental.pallas import tpu as pltpu
from jax.sharding import PartitionSpec as P

BLOCK = 64
NNZ = 8
LEVELS = 2
F32, BF16 = jnp.float32, jnp.bfloat16
NN = ((1,), (0,))
NT = ((1,), (1,))
TN = ((0,), (0,))
MESH = pl.DeviceIdType.MESH
VMEM_LIMIT = 48 * 1024 * 1024


def split(a):
    hi = a.astype(BF16)
    return hi, (a - hi.astype(F32)).astype(BF16)

def mm(a, b, dims=((1,), (0,))):
    return lax.dot_general(a, b, (dims, ((), ())), preferred_element_type=F32)


def mm3(a, b, dims=NN):
    ah, al = split(a)
    bh, bl = split(b)
    return mm(ah, bh, dims) + (mm(ah, bl, dims) + mm(al, bh, dims))

def leaf(aq, W=32):
    T = W // 8
    def panel(k, _):
        r0 = pl.multiple_of(k * W, W)
        rows = aq[pl.ds(r0, W), :]
        diag = pltpu.roll(rows[:, :128], lax.rem(128 - r0, 128), axis=1)
        C = [[jnp.broadcast_to(diag[8*t:8*t+8, m:m+1], (8, 128)) for t in range(T)] for m in range(W)]
        lane = lax.broadcasted_iota(jnp.int32, (8, 128), 1)
        sub = lax.broadcasted_iota(jnp.int32, (8, 128), 0)
        E = [(lane == sub + 8*t).astype(F32) for t in range(T)]
        scale = [jnp.zeros((8, 128), F32) for t in range(T)]
        for j in range(W):
            tj, sj = divmod(j, 8)
            piv = jnp.broadcast_to(C[j][tj][sj:sj+1, :], (8, 128))
            r = pl.reciprocal(piv, approx=True)
            f = [None]*T
            for t in range(tj, T):
                f[t] = C[j][t] * r
            f[tj] = jnp.where(sub > sj, f[tj], 0.0)
            for m in range(j + 1, W):
                tm, sm = divmod(m, 8)
                c = jnp.broadcast_to(C[j][tm][sm:sm+1, :], (8, 128))
                for t in range(tm, T):
                    C[m][t] = C[m][t] - f[t] * c
            e = jnp.broadcast_to(E[tj][sj:sj+1, :], (8, 128))
            for t in range(tj, T):
                E[t] = E[t] - f[t] * e
            scale[tj] = jnp.where(sub == sj, piv, scale[tj])
        E = [E[t] * lax.rsqrt(scale[t]) for t in range(T)]
        inv = jnp.concatenate(E, 0)[:, :W]
        R = mm3(inv, rows)
        low = jnp.transpose(R[:, :128])
        low = jnp.where(lax.broadcasted_iota(jnp.int32, low.shape, 0) >= r0 + W, low, 0.0)
        aq[...] = aq[...] - mm3(low, R)
        aq[pl.ds(r0, W), :] = R
        return 0
    lax.fori_loop(0, 128 // W, panel, 0)

def chol_upper(a, z, aq):
    ident = eye(128)
    aq[:, 128:] = ident
    aq[:, :128] = a[:128, :128]
    leaf(aq)
    z11 = aq[:, 128:]
    z[:128, :128] = z11
    l21 = mm3(a[128:, :128], z11, NT)
    aq[:, :128] = a[128:, 128:] - mm3(l21, l21, NT)
    aq[:, 128:] = ident
    z[128:, :128] = mm3(l21, z11)


def chol_lower(z, aq):
    leaf(aq)
    z22 = aq[:, 128:]
    z[128:, 128:] = z22
    z[128:, :128] = -mm3(z22, z[128:, :128])
    z[:128, 128:] = jnp.zeros((128, 128), F32)


def chol_inv(a, z, aq):
    chol_upper(a, z, aq)
    chol_lower(z, aq)


def iota(shape, dim):
    return lax.broadcasted_iota(jnp.int32, shape, dim)


def eye(n):
    return (iota((n, n), 0) == iota((n, n), 1)).astype(F32)


def mm3s(a, b, dims=NN):
    return mm(a[0], b[0], dims) + (mm(a[0], b[1], dims) + mm(a[1], b[0], dims))


def mm2(a, b, dims=NN):
    high, low = split(a)
    return mm(high, b, dims) + mm(low, b, dims)


def mm2r(a, b, dims=NN):
    high, low = split(b)
    return mm(a, high, dims) + mm(a, low, dims)


def newton_step(a_ref, z_ref):
    a = a_ref[...]
    row, col = iota(a.shape, 0), iota(a.shape, 1)
    h = split(jnp.where(row > col, -a, jnp.where(row == col, 1.5 - 0.5 * a, 0.0)))
    t = mm3s(h, split(a))
    z = mm3s(h, split(z_ref[...]))
    a_ref[...] = mm3s(split(t), h, NT)
    z_ref[...] = z


def residual(a, count):
    worst = jnp.float32(0.0)
    for i in range(count):
        off = a[i] - eye(a.shape[1])
        total = jnp.sum(off * off)
        worst = jnp.maximum(worst, jnp.where(total < 1e30, total, 1e30))
    return worst


def factor(a, z, first, start, wide, count, fixed, most):
    for i in range(count):
        first[i] = a[i]
        start[i] = z[i]
    for _ in range(fixed):
        for i in range(count):
            newton_step(a.at[i], z.at[i])

    def unsettled(state):
        return jnp.logical_and(state[0] < most, state[1] > 3e-5)

    def again(state):
        for i in range(count):
            newton_step(a.at[i], z.at[i])
        return state[0] + 1, residual(a, count)

    left = lax.while_loop(unsettled, again, (jnp.int32(fixed), residual(a, count)))[1]

    @pl.when(left > 3e-5)
    def _():
        def direct(i, _):
            chol_inv(first.at[i], z.at[i], wide)
            z[i] = mm3(z[i], start[i])
            return 0

        lax.fori_loop(0, count, direct, 0)


class Phases:
    def __init__(self, sends, arrivals):
        self.sends, self.arrivals = sends, arrivals
        self.flying = []
        me = lax.axis_index("space")
        self.core = lax.rem(me, 2)
        self.y = lax.rem(me // 2, 4)
        self.x = me // 8
        self.snap = lax.axis_index("snap")
        self.place = lax.rem(self.snap, 4)
        self.used = 0

    def space(self, x, y, core):
        return (x * 4 + y) * 2 + core

    def peers(self):
        found = [{"space": self.space(self.x, self.y, 1 - self.core)}]
        for d in (1, 2, 3):
            found.append({"space": self.space(lax.rem(self.x + d, 4), self.y, self.core)})
            found.append({"space": self.space(self.x, lax.rem(self.y + d, 4), self.core)})
            found.append({"snap": self.other(d)})
        return found

    def other(self, d):
        place = self.place
        if d & 1:
            place = place + 1 - 2 * lax.rem(place, 2)
        if d & 2:
            place = place + 2 - 4 * (place // 2)
        return self.snap - self.place + place

    def send(self, src, dst, device):
        slot = self.used
        self.used += 1
        copy = pltpu.make_async_remote_copy(
            src_ref=src,
            dst_ref=dst,
            send_sem=self.sends.at[slot],
            recv_sem=self.arrivals.at[slot],
            device_id=device,
            device_id_type=MESH,
        )
        copy.start()
        self.flying.append(copy)
        return copy

    def finish(self):
        for copy in self.flying:
            copy.wait_send()

    def greet(self, devices):
        barrier = pltpu.get_barrier_semaphore()
        for device in devices:
            pl.semaphore_signal(barrier, inc=1, device_id=device, device_id_type=MESH)

    def met(self, count):
        pl.semaphore_wait(pltpu.get_barrier_semaphore(), count)

    def along(self, half, major, d):
        if (half == 0) == major:
            place = lax.rem(self.x + d, 4)
            return place, {"space": self.space(place, self.y, self.core)}
        place = lax.rem(self.y + d, 4)
        return place, {"space": self.space(self.x, place, self.core)}

    def own(self, half, major):
        return self.x if (half == 0) == major else self.y


def rows_of(place, size):
    return pl.ds(pl.multiple_of(place * size, size), size)


def sum_over_space(ph, part, bc, bx, by, s1, s2, s3, spread, beside=None):
    copy = ph.send(
        part.at[:, :, rows_of(1 - ph.core, 128), :],
        bc,
        {"space": ph.space(ph.x, ph.y, 1 - ph.core)},
    )
    copy.wait_recv()
    s1[...] = part[:, :, rows_of(ph.core, 128), :] + bc[...]
    copies = []
    for d in (1, 2, 3):
        for half in (0, 1):
            place, device = ph.along(half, True, d)
            copies.append(ph.send(s1.at[half, :, rows_of(place, 32), :], bx.at[half, d - 1], device))
    if beside is not None:
        beside()
    for copy in copies:
        copy.wait_recv()
    for half in (0, 1):
        mine = s1[half, :, rows_of(ph.own(half, True), 32), :]
        s2[half] = mine + (bx[half, 0] + bx[half, 1] + bx[half, 2])
    copies = []
    for d in (1, 2, 3):
        for half in (0, 1):
            place, device = ph.along(half, False, d)
            copies.append(ph.send(s2.at[half, :, rows_of(place, 8), :], by.at[half, d - 1], device))
    for copy in copies:
        copy.wait_recv()
    for half in (0, 1):
        mine = s2[half, :, rows_of(ph.own(half, False), 8), :]
        s3[half] = mine + (by[half, 0] + by[half, 1] + by[half, 2])
    copies = []
    for d in (1, 2, 3):
        copies.append(ph.send(s3, spread.at[d], {"snap": ph.other(d)}))
    spread[0] = s3[...]
    for copy in copies:
        copy.wait_recv()


def give_over_space(ph, chunk, g1, g2, out, beside=None):
    copies = []
    for half in (0, 1):
        mine = rows_of(ph.own(half, False), 8)
        for d in (1, 2, 3):
            _, device = ph.along(half, False, d)
            copies.append(ph.send(chunk.at[half], g1.at[half, :, mine, :], device))
        g1[half, :, mine, :] = chunk[half]
    for copy in copies:
        copy.wait_recv()
    copies = []
    for half in (0, 1):
        mine = rows_of(ph.own(half, True), 32)
        for d in (1, 2, 3):
            _, device = ph.along(half, True, d)
            copies.append(ph.send(g1.at[half], g2.at[half, :, mine, :], device))
        g2[half, :, mine, :] = g1[half]
    if beside is not None:
        beside()
    for copy in copies:
        copy.wait_recv()
    mine = rows_of(ph.core, 128)
    copy = ph.send(
        g2, out.at[:, :, mine, :], {"space": ph.space(ph.x, ph.y, 1 - ph.core)}
    )
    out[:, :, mine, :] = g2[...]
    copy.wait_recv()


def put_halves(ref, index, square):
    ref[0, index] = square[:, :128]
    ref[1, index] = square[:, 128:]


def whole(ref, index):
    return jnp.concatenate([ref[0, index], ref[1, index]], axis=1)


def quarter_rows(place, size):
    return rows_of(2 * lax.rem(place, 2) + place // 2, size)


def first_sum(
    count_ref, x_ref, volume_ref, om_ref, out_ref, parts_ref, zo_ref,
    part, bc, bx, by, s1, s2, s3, spread, chunk, g1, g2, got, sends, arrivals, local, parts, m, zo, wide
):
    ph = Phases(sends, arrivals)
    ph.greet(ph.peers())
    used = count_ref[0] * BLOCK
    local[...] = jnp.where(iota(x_ref.shape, 0) < used, x_ref[...], 0)
    total = x_ref.shape[0] * lax.axis_size("space")
    weight = jnp.where(iota(volume_ref.shape, 1) < used, volume_ref[...], 0.0) / total
    weighted = jnp.transpose(local[...]).astype(F32) * weight
    put_halves(part, 0, mm2(weighted, local[...]))
    ph.met(10)
    quarter = parts.shape[1]

    def give_rows(d):
        there = ph.other(d)
        rows = quarter_rows(lax.rem(there, 4), quarter)
        return ph.send(local.at[rows, :], parts.at[d - 1], {"snap": there})

    bulk = [give_rows(2), give_rows(1)]
    om = om_ref[ph.core]
    m[...] = mm(om, om, TN)
    mine = zo.at[ph.core]
    sum_over_space(
        ph, part, bc, bx, by, s1, s2, s3, spread, lambda: chol_upper(m, mine, wide)
    )
    bulk.append(give_rows(3))
    for d in range(4):
        chunk[:, d] = spread[d, :, 0]
    give_over_space(ph, chunk, g1, g2, got, lambda: chol_lower(mine, wide))
    factor_copy = ph.send(mine, mine, {"space": ph.space(ph.x, ph.y, 1 - ph.core)})
    for d in range(4):
        out_ref[d] = whole(got, d)
    parts_ref[0] = local[quarter_rows(ph.place, quarter), :]
    for d, copy in zip((2, 1, 3), bulk):
        copy.wait_recv()
        parts_ref[d] = parts[d - 1]
    factor_copy.wait_recv()
    zo_ref[...] = zo[...]
    ph.finish()


def gram_factors(g_ref, z, a, first, start, wide):
    rank = g_ref.shape[1]
    diagonal = iota((rank, rank), 0) == iota((rank, rank), 1)
    for d in range(4):
        g = g_ref[d]
        pivots = jnp.where(diagonal, g, 0.0)
        down = lax.rsqrt(jnp.sum(pivots, axis=1, keepdims=True))
        across = lax.rsqrt(jnp.sum(pivots, axis=0, keepdims=True))
        a[d] = g * down * across
        z[d] = jnp.where(diagonal, down, 0.0)
    factor(a, z, first, start, wide, 4, 3, 8)


def second_sum(
    count_ref, z_ref, x_ref, volume_ref, om_ref, out_ref, sk_ref,
    part, bc, bx, by, s1, s2, s3, spread, chunk, g1, g2, got, sends, arrivals, base, sketch
):
    ph = Phases(sends, arrivals)
    ph.greet(ph.peers())
    rank = om_ref.shape[2]
    quarter = x_ref.shape[1]
    for d in range(4):
        base[lax.rem(ph.other(d), 4)] = mm2r(x_ref[d], z_ref[d], NT).astype(BF16)
    start = quarter_rows(ph.place, quarter)
    used = count_ref[0] * BLOCK
    lanes = iota((1, quarter), 1) + (2 * lax.rem(ph.place, 2) + ph.place // 2) * quarter
    total = 4 * quarter * lax.axis_size("space")
    weight = jnp.where(lanes < used, volume_ref[:, start], 0.0) / total
    mine = sketch.at[ph.place // 2]
    for pair in (0, 1):
        low, high = base[2 * pair], base[2 * pair + 1]
        both = mm(low, om_ref[0, :rank, :]) + mm(high, om_ref[0, rank:, :])
        mine[:, pair * rank : (pair + 1) * rank] = both.astype(BF16)
        put_halves(part, pair, mm2(jnp.transpose(low).astype(F32) * weight, high))
    low, high = mine[:, :rank], mine[:, rank:]
    put_halves(part, 2, mm2(jnp.transpose(low).astype(F32) * weight, high))
    ph.met(10)
    far = {"snap": ph.other(2)}
    piece = quarter // 2

    def give_sketch(i):
        rows = mine.at[pl.ds(i * piece, piece), :]
        return ph.send(rows, rows, far)

    bulk = [give_sketch(0)]
    sum_over_space(ph, part, bc, bx, by, s1, s2, s3, spread)
    bulk.append(give_sketch(1))
    chunk[...] = (spread[0] + spread[1]) + (spread[2] + spread[3])
    give_over_space(ph, chunk, g1, g2, got)
    for d in range(3):
        out_ref[d] = whole(got, d)
    for copy in bulk:
        copy.wait_recv()
    sk_ref[...] = sketch[...].reshape(sk_ref.shape)
    ph.finish()


def sum_scratch(before, after, copies=29):
    return [
        pltpu.VMEM((2, before, 128, 128), F32),
        pltpu.VMEM((2, 3, before, 32, 128), F32),
        pltpu.VMEM((2, 3, before, 8, 128), F32),
        pltpu.VMEM((2, before, 128, 128), F32),
        pltpu.VMEM((2, before, 32, 128), F32),
        pltpu.VMEM((2, before, 8, 128), F32),
        pltpu.VMEM((4, 2, before, 8, 128), F32),
        pltpu.VMEM((2, after, 8, 128), F32),
        pltpu.VMEM((2, after, 32, 128), F32),
        pltpu.VMEM((2, after, 128, 128), F32),
        pltpu.VMEM((2, after, 256, 128), F32),
        pltpu.SemaphoreType.DMA((copies,)),
        pltpu.SemaphoreType.DMA((copies,)),
    ]


def near_identity(z, om, cross, a, t):
    rank = cross.shape[0]
    qa = mm2(z, om[:rank], NT)
    qb = mm2r(om[rank:], z, NT)
    t[...] = mm3(qa, mm3(cross, qb))
    a[...] = eye(rank) + t[...] + jnp.transpose(t[...])


def merge_factors(c_ref, om_ref, zo_ref, out_ref, a, z, first, start, t, wide):
    rank = om_ref.shape[2]
    for pair in (0, 1):
        near_identity(zo_ref[0], om_ref[0], c_ref[pair], a.at[pair], t.at[pair])
        z[pair] = zo_ref[0]
    factor(a, z, first, start, wide, 2, 3, 8)
    cross = mm3(mm3(z[0], c_ref[2]), z[1], NT)
    near_identity(zo_ref[1], om_ref[1], cross, a.at[2], t.at[0])
    z[2] = zo_ref[1]
    factor(a.at[pl.ds(2, 1)], z.at[pl.ds(2, 1)], first, start, wide, 1, 3, 8)
    last = z[2]
    for pair in (0, 1):
        u = mm2r(om_ref[1, pair * rank : (pair + 1) * rank, :], last, NT)
        out_ref[pair * rank : (pair + 1) * rank, :] = mm3(jnp.transpose(z[pair]), u)


def spread_kernel(
    rim_ref, sk_ref, mix_ref, base_ref, rims_ref, own, base, rim_out, rim_in, sends, arrivals
):
    ph = Phases(sends, arrivals)
    me, n = lax.axis_index("space"), lax.axis_size("space")
    near = ph.other(1)
    before, after = lax.rem(me + n - 1, n), lax.rem(me + 1, n)
    targets = [{"space": before}, {"space": after}]
    targets += [{"space": before, "snap": near}, {"space": after, "snap": near}]
    ph.greet([{"snap": near}] + targets)
    high, low = split(mix_ref[...])
    half = base.shape[0] // 2
    upper = lax.rem(ph.place, 2)
    pieces = 4
    size = half // pieces
    for piece in range(pieces):
        rows = slice(piece * size * BLOCK, (piece + 1) * size * BLOCK)
        sk = sk_ref[rows, :]
        found = (mm(sk, high) + mm(sk, low)).astype(BF16)
        own[piece * size : (piece + 1) * size] = found.reshape(size, *own.shape[1:])
    ph.met(5)
    mine = base.at[pl.ds(upper * half, half)]
    copy = ph.send(own, mine, {"snap": near})
    for side in (0, 1):
        where = rim_ref[0, side] - upper * half
        block = own[jnp.clip(where, 0, half - 1)]
        inside = jnp.logical_and(where >= 0, where < half)
        rim_out[side] = jnp.where(inside, block, jnp.zeros_like(block))
    swaps = [
        ph.send(rim_out.at[0], rim_in.at[1, 0], targets[0]),
        ph.send(rim_out.at[1], rim_in.at[0, 0], targets[1]),
        ph.send(rim_out.at[0], rim_in.at[1, 1], targets[2]),
        ph.send(rim_out.at[1], rim_in.at[0, 1], targets[3]),
    ]
    base[pl.ds(upper * half, half)] = own[...]
    for swap in swaps:
        swap.wait_recv()
    rims_ref[:BLOCK, :] = jnp.where(me > 0, rim_in[0, 0] + rim_in[0, 1], 0)
    rims_ref[BLOCK:, :] = jnp.where(me < n - 1, rim_in[1, 0] + rim_in[1, 1], 0)
    copy.wait_recv()
    base_ref[...] = base[...].reshape(base_ref.shape)
    ph.finish()


def product_kernel(cols_ref, count_ref, full_ref, rims_ref, jac_ref, base_ref, out_ref, held):
    rows, rank = full_ref.shape
    blocks = rows // BLOCK
    base_ref[...] = full_ref[...]
    held[:rows, :] = full_ref[...]
    held[rows:, :] = rims_ref[...]
    count = count_ref[0]

    def block(b, _):
        here = pl.ds(pl.multiple_of(b * BLOCK, BLOCK), BLOCK)
        picked = [
            held[pl.ds(pl.multiple_of(cols_ref[b, k] * BLOCK, BLOCK), BLOCK), :] for k in range(NNZ)
        ]
        product = mm(jac_ref[here, :], jnp.concatenate(picked, axis=0))
        out_ref[here, :] = jnp.where(b < count, product, 0.0).astype(BF16)
        return 0

    lax.fori_loop(0, blocks, block, 0, unroll=2)


VM = pl.BlockSpec(memory_space=pltpu.VMEM)
SM = pl.BlockSpec(memory_space=pltpu.SMEM)


def call(body, outs, ins, scratch, name, **params):
    return pl.pallas_call(
        body,
        out_shape=outs,
        in_specs=ins,
        out_specs=jax.tree.map(lambda _: VM, outs),
        scratch_shapes=scratch,
        compiler_params=pltpu.CompilerParams(vmem_limit_bytes=VMEM_LIMIT, **params),
        name=name,
    )


def on_device(snapshots, cell_volume, counts, rim_rows, jac_cols, jacobian, omega):
    rows, rank = snapshots.shape
    blocks, quarter = rows // BLOCK, rows // 4
    volume = cell_volume.reshape(1, rows)
    square = (rank, rank)
    wide = pltpu.VMEM((rank // 2, rank), F32)

    def squares(n):
        return pltpu.VMEM((n, rank, rank), F32)

    grams, parts, starts = call(
        first_sum,
        [
            jax.ShapeDtypeStruct((4, rank, rank), F32),
            jax.ShapeDtypeStruct((4, quarter, rank), BF16),
            jax.ShapeDtypeStruct((2, rank, rank), F32),
        ],
        [SM] + [VM] * 3,
        [pltpu.VMEM((2, 1, rank, rank // 2), F32)]
        + sum_scratch(1, 4, 33)
        + [
            pltpu.VMEM((rows, rank), BF16),
            pltpu.VMEM((3, quarter, rank), BF16),
            pltpu.VMEM(square, F32),
            squares(2),
            wide,
        ],
        "first_sum",
        collective_id=0,
        has_side_effects=True,
    )(counts, snapshots, volume, omega)
    factors = call(
        gram_factors,
        jax.ShapeDtypeStruct((4, rank, rank), F32),
        [VM],
        [squares(4)] * 3 + [wide],
        "gram_factors",
    )(grams)
    cross, sketch = call(
        second_sum,
        [
            jax.ShapeDtypeStruct((3, rank, rank), F32),
            jax.ShapeDtypeStruct((2 * quarter, 2 * rank), BF16),
        ],
        [SM] + [VM] * 4,
        [pltpu.VMEM((2, 3, rank, rank // 2), F32)]
        + sum_scratch(3, 3, 31)
        + [pltpu.VMEM((4, quarter, rank), BF16), pltpu.VMEM((2, quarter, 2 * rank), BF16)],
        "second_sum",
        collective_id=1,
        has_side_effects=True,
    )(counts, factors, parts, volume, omega)
    mix = call(
        merge_factors,
        jax.ShapeDtypeStruct((2 * rank, rank), F32),
        [VM] * 3,
        [squares(3), squares(3), squares(2), squares(2), squares(2), wide],
        "merge_factors",
    )(cross, omega, starts)
    full, rims = call(
        spread_kernel,
        [
            jax.ShapeDtypeStruct((rows, rank), BF16),
            jax.ShapeDtypeStruct((2 * BLOCK, rank), BF16),
        ],
        [SM, VM, VM],
        [
            pltpu.VMEM((blocks // 2, BLOCK, rank), BF16),
            pltpu.VMEM((blocks, BLOCK, rank), BF16),
            pltpu.VMEM((2, BLOCK, rank), BF16),
            pltpu.VMEM((2, 2, BLOCK, rank), BF16),
            pltpu.SemaphoreType.DMA((5,)),
            pltpu.SemaphoreType.DMA((5,)),
        ],
        "spread_rows",
        collective_id=2,
        has_side_effects=True,
    )(rim_rows, sketch, mix)
    basis, product = call(
        product_kernel,
        [jax.ShapeDtypeStruct((rows, rank), BF16)] * 2,
        [SM, SM, VM, VM, VM],
        [pltpu.VMEM((rows + 2 * BLOCK, rank), BF16)],
        "jac_product",
    )(jac_cols, counts, full, rims, jacobian)
    return (basis, product)


def solution(mesh):
    in_specs = (
        P("space", "snap"),
        P("space"),
        P("space"),
        P("space", None),
        P("space", None),
        P("space", None),
        P(),
    )
    out_specs = (P("space", "snap"), P("space", "snap"))
    return jax.shard_map(
        on_device, mesh=mesh, in_specs=in_specs, out_specs=out_specs, check_vma=False
    )
```

```python
import functools

import jax
import jax.numpy as jnp
from jax import lax
from jax.experimental import pallas as pl
from jax.experimental.pallas import tpu as pltpu
from jax.sharding import PartitionSpec as P

BLOCK = 64
NNZ = 8
LEVELS = 2
F32, BF16 = jnp.float32, jnp.bfloat16
NN = ((1,), (0,))
NT = ((1,), (1,))
TN = ((0,), (0,))
MESH = pl.DeviceIdType.MESH
VMEM_LIMIT = 48 * 1024 * 1024


def split(a):
    hi = a.astype(BF16)
    return hi, (a - hi.astype(F32)).astype(BF16)

def mm(a, b, dims=((1,), (0,))):
    return lax.dot_general(a, b, (dims, ((), ())), preferred_element_type=F32)


def mm3(a, b, dims=NN):
    ah, al = split(a)
    bh, bl = split(b)
    return mm(ah, bh, dims) + (mm(ah, bl, dims) + mm(al, bh, dims))

def leaf(aq, W=32):
    T = W // 8
    def panel(k, _):
        r0 = pl.multiple_of(k * W, W)
        rows = aq[pl.ds(r0, W), :]
        diag = pltpu.roll(rows[:, :128], lax.rem(128 - r0, 128), axis=1)
        C = [[jnp.broadcast_to(diag[8*t:8*t+8, m:m+1], (8, 128)) for t in range(T)] for m in range(W)]
        lane = lax.broadcasted_iota(jnp.int32, (8, 128), 1)
        sub = lax.broadcasted_iota(jnp.int32, (8, 128), 0)
        E = [(lane == sub + 8*t).astype(F32) for t in range(T)]
        scale = [jnp.zeros((8, 128), F32) for t in range(T)]
        for j in range(W):
            tj, sj = divmod(j, 8)
            piv = jnp.broadcast_to(C[j][tj][sj:sj+1, :], (8, 128))
            r = pl.reciprocal(piv, approx=True)
            f = [None]*T
            for t in range(tj, T):
                f[t] = C[j][t] * r
            f[tj] = jnp.where(sub > sj, f[tj], 0.0)
            for m in range(j + 1, W):
                tm, sm = divmod(m, 8)
                c = jnp.broadcast_to(C[j][tm][sm:sm+1, :], (8, 128))
                for t in range(tm, T):
                    C[m][t] = C[m][t] - f[t] * c
            e = jnp.broadcast_to(E[tj][sj:sj+1, :], (8, 128))
            for t in range(tj, T):
                E[t] = E[t] - f[t] * e
            scale[tj] = jnp.where(sub == sj, piv, scale[tj])
        E = [E[t] * lax.rsqrt(scale[t]) for t in range(T)]
        inv = jnp.concatenate(E, 0)[:, :W]
        R = mm3(inv, rows)
        low = jnp.transpose(R[:, :128])
        low = jnp.where(lax.broadcasted_iota(jnp.int32, low.shape, 0) >= r0 + W, low, 0.0)
        aq[...] = aq[...] - mm3(low, R)
        aq[pl.ds(r0, W), :] = R
        return 0
    lax.fori_loop(0, 128 // W, panel, 0)

def chol_upper(a, z, aq):
    ident = eye(128)
    aq[:, 128:] = ident
    aq[:, :128] = a[:128, :128]
    leaf(aq)
    z11 = aq[:, 128:]
    z[:128, :128] = z11
    l21 = mm3(a[128:, :128], z11, NT)
    aq[:, :128] = a[128:, 128:] - mm3(l21, l21, NT)
    aq[:, 128:] = ident
    z[128:, :128] = mm3(l21, z11)


def chol_lower(z, aq):
    leaf(aq)
    z22 = aq[:, 128:]
    z[128:, 128:] = z22
    z[128:, :128] = -mm3(z22, z[128:, :128])
    z[:128, 128:] = jnp.zeros((128, 128), F32)


def chol_inv(a, z, aq):
    chol_upper(a, z, aq)
    chol_lower(z, aq)


def iota(shape, dim):
    return lax.broadcasted_iota(jnp.int32, shape, dim)


def eye(n):
    return (iota((n, n), 0) == iota((n, n), 1)).astype(F32)


def mm3s(a, b, dims=NN):
    return mm(a[0], b[0], dims) + (mm(a[0], b[1], dims) + mm(a[1], b[0], dims))


def mm2(a, b, dims=NN):
    high, low = split(a)
    return mm(high, b, dims) + mm(low, b, dims)


def mm2r(a, b, dims=NN):
    high, low = split(b)
    return mm(a, high, dims) + mm(a, low, dims)


def newton_step(a_ref, z_ref, rough=False):
    a = a_ref[...]
    row, col = iota(a.shape, 0), iota(a.shape, 1)
    h = jnp.where(row > col, -a, jnp.where(row == col, 1.5 - 0.5 * a, 0.0))
    if rough:
        h = h.astype(BF16)
        t = mm2r(h, a)
        z = mm2r(h, z_ref[...])
        a_ref[...] = mm2(t, h, NT)
        z_ref[...] = z
        return
    h = split(h)
    t = mm3s(h, split(a))
    z = mm3s(h, split(z_ref[...]))
    a_ref[...] = mm3s(split(t), h, NT)
    z_ref[...] = z


def residual(a, count):
    worst = jnp.float32(0.0)
    for i in range(count):
        off = a[i] - eye(a.shape[1])
        total = jnp.sum(off * off)
        worst = jnp.maximum(worst, jnp.where(total < 1e30, total, 1e30))
    return worst


def factor(a, z, first, start, wide, count, fixed, most):
    for i in range(count):
        first[i] = a[i]
        start[i] = z[i]
    for step in range(fixed):
        for i in range(count):
            newton_step(a.at[i], z.at[i], step < 2)

    def unsettled(state):
        return jnp.logical_and(state[0] < most, state[1] > 3e-5)

    def again(state):
        for i in range(count):
            newton_step(a.at[i], z.at[i])
        return state[0] + 1, residual(a, count)

    left = lax.while_loop(unsettled, again, (jnp.int32(fixed), residual(a, count)))[1]

    @pl.when(left > 3e-5)
    def _():
        def direct(i, _):
            chol_inv(first.at[i], z.at[i], wide)
            z[i] = mm3(z[i], start[i])
            return 0

        lax.fori_loop(0, count, direct, 0)


class Phases:
    def __init__(self, sends, arrivals):
        self.sends, self.arrivals = sends, arrivals
        self.flying = []
        me = lax.axis_index("space")
        self.core = lax.rem(me, 2)
        self.y = lax.rem(me // 2, 4)
        self.x = me // 8
        self.snap = lax.axis_index("snap")
        self.place = lax.rem(self.snap, 4)
        self.used = 0

    def space(self, x, y, core):
        return (x * 4 + y) * 2 + core

    def peers(self):
        found = [{"space": self.space(self.x, self.y, 1 - self.core)}]
        for d in (1, 2, 3):
            found.append({"space": self.space(lax.rem(self.x + d, 4), self.y, self.core)})
            found.append({"space": self.space(self.x, lax.rem(self.y + d, 4), self.core)})
            found.append({"snap": self.other(d)})
        return found

    def other(self, d):
        place = self.place
        if d & 1:
            place = place + 1 - 2 * lax.rem(place, 2)
        if d & 2:
            place = place + 2 - 4 * (place // 2)
        return self.snap - self.place + place

    def send(self, src, dst, device):
        slot = self.used
        self.used += 1
        copy = pltpu.make_async_remote_copy(
            src_ref=src,
            dst_ref=dst,
            send_sem=self.sends.at[slot],
            recv_sem=self.arrivals.at[slot],
            device_id=device,
            device_id_type=MESH,
        )
        copy.start()
        self.flying.append(copy)
        return copy

    def finish(self):
        for copy in self.flying:
            copy.wait_send()

    def greet(self, devices):
        barrier = pltpu.get_barrier_semaphore()
        for device in devices:
            pl.semaphore_signal(barrier, inc=1, device_id=device, device_id_type=MESH)

    def met(self, count):
        pl.semaphore_wait(pltpu.get_barrier_semaphore(), count)

    def along(self, half, major, d):
        if (half == 0) == major:
            place = lax.rem(self.x + d, 4)
            return place, {"space": self.space(place, self.y, self.core)}
        place = lax.rem(self.y + d, 4)
        return place, {"space": self.space(self.x, place, self.core)}

    def own(self, half, major):
        return self.x if (half == 0) == major else self.y


def rows_of(place, size):
    return pl.ds(pl.multiple_of(place * size, size), size)


def sum_over_space(ph, part, bc, bx, by, s1, s2, s3, spread, beside=None):
    copy = ph.send(
        part.at[:, :, rows_of(1 - ph.core, 128), :],
        bc,
        {"space": ph.space(ph.x, ph.y, 1 - ph.core)},
    )
    copy.wait_recv()
    s1[...] = part[:, :, rows_of(ph.core, 128), :] + bc[...]
    copies = []
    for d in (1, 2, 3):
        for half in (0, 1):
            place, device = ph.along(half, True, d)
            copies.append(ph.send(s1.at[half, :, rows_of(place, 32), :], bx.at[half, d - 1], device))
    if beside is not None:
        beside()
    for copy in copies:
        copy.wait_recv()
    for half in (0, 1):
        mine = s1[half, :, rows_of(ph.own(half, True), 32), :]
        s2[half] = mine + (bx[half, 0] + bx[half, 1] + bx[half, 2])
    copies = []
    for d in (1, 2, 3):
        for half in (0, 1):
            place, device = ph.along(half, False, d)
            copies.append(ph.send(s2.at[half, :, rows_of(place, 8), :], by.at[half, d - 1], device))
    for copy in copies:
        copy.wait_recv()
    for half in (0, 1):
        mine = s2[half, :, rows_of(ph.own(half, False), 8), :]
        s3[half] = mine + (by[half, 0] + by[half, 1] + by[half, 2])
    copies = []
    for d in (1, 2, 3):
        copies.append(ph.send(s3, spread.at[d], {"snap": ph.other(d)}))
    spread[0] = s3[...]
    for copy in copies:
        copy.wait_recv()


def give_over_space(ph, chunk, g1, g2, out, beside=None):
    copies = []
    for half in (0, 1):
        mine = rows_of(ph.own(half, False), 8)
        for d in (1, 2, 3):
            _, device = ph.along(half, False, d)
            copies.append(ph.send(chunk.at[half], g1.at[half, :, mine, :], device))
        g1[half, :, mine, :] = chunk[half]
    for copy in copies:
        copy.wait_recv()
    copies = []
    for half in (0, 1):
        mine = rows_of(ph.own(half, True), 32)
        for d in (1, 2, 3):
            _, device = ph.along(half, True, d)
            copies.append(ph.send(g1.at[half], g2.at[half, :, mine, :], device))
        g2[half, :, mine, :] = g1[half]
    if beside is not None:
        beside()
    for copy in copies:
        copy.wait_recv()
    mine = rows_of(ph.core, 128)
    copy = ph.send(
        g2, out.at[:, :, mine, :], {"space": ph.space(ph.x, ph.y, 1 - ph.core)}
    )
    out[:, :, mine, :] = g2[...]
    copy.wait_recv()


def put_halves(ref, index, square):
    ref[0, index] = square[:, :128]
    ref[1, index] = square[:, 128:]


def whole(ref, index):
    return jnp.concatenate([ref[0, index], ref[1, index]], axis=1)


def quarter_rows(place, size):
    return rows_of(2 * lax.rem(place, 2) + place // 2, size)


def first_sum(
    count_ref, x_ref, volume_ref, om_ref, out_ref, parts_ref, zo_ref, weight_ref,
    part, bc, bx, by, s1, s2, s3, spread, chunk, g1, g2, got, sends, arrivals,
    raw, om_local, loads, local, parts, m, zo, wide
):
    ph = Phases(sends, arrivals)
    load = pltpu.make_async_copy(x_ref, raw, loads.at[0])
    load.start()
    om_load = pltpu.make_async_copy(om_ref.at[ph.core], om_local, loads.at[1])
    om_load.start()
    ph.greet(ph.peers())
    used = count_ref[0] * BLOCK
    rows = raw.shape[0]
    total = rows * lax.axis_size("space")
    volume = volume_ref[...].reshape(1, rows)
    weight = jnp.where(iota((1, rows), 1) < used, volume, 0.0) / total
    weight_ref[...] = weight
    load.wait()
    local[...] = jnp.where(iota(raw.shape, 0) < used, raw[...], 0)
    weighted = jnp.transpose(local[...]).astype(F32) * weight
    put_halves(part, 0, mm2(weighted, local[...]))
    ph.met(10)
    quarter = parts.shape[1]

    def give_rows(d):
        there = ph.other(d)
        rows = quarter_rows(lax.rem(there, 4), quarter)
        return ph.send(local.at[rows, :], parts.at[d - 1], {"snap": there})

    bulk = [give_rows(2), give_rows(1)]
    om_load.wait()
    om = om_local[...]
    m[...] = mm(om, om, TN)
    mine = zo.at[ph.core]
    sum_over_space(
        ph, part, bc, bx, by, s1, s2, s3, spread, lambda: chol_upper(m, mine, wide)
    )
    bulk.append(give_rows(3))
    for d in range(4):
        chunk[:, d] = spread[d, :, 0]
    give_over_space(ph, chunk, g1, g2, got, lambda: chol_lower(mine, wide))
    factor_copy = ph.send(mine, mine, {"space": ph.space(ph.x, ph.y, 1 - ph.core)})
    for d in range(4):
        out_ref[d] = whole(got, d)
    parts_ref[0] = local[quarter_rows(ph.place, quarter), :]
    for d, copy in zip((2, 1, 3), bulk):
        copy.wait_recv()
        parts_ref[d] = parts[d - 1]
    factor_copy.wait_recv()
    zo_ref[...] = zo[...]
    ph.finish()


def gram_factors(g_ref, z, a, first, start, wide):
    rank = g_ref.shape[1]
    diagonal = iota((rank, rank), 0) == iota((rank, rank), 1)
    for d in range(4):
        g = g_ref[d]
        pivots = jnp.where(diagonal, g, 0.0)
        down = lax.rsqrt(jnp.sum(pivots, axis=1, keepdims=True))
        across = lax.rsqrt(jnp.sum(pivots, axis=0, keepdims=True))
        a[d] = g * down * across
        z[d] = jnp.where(diagonal, down, 0.0)
    factor(a, z, first, start, wide, 4, 3, 8)


def second_sum(
    z_ref, x_ref, weight_ref, om_ref, zo_ref, out_ref, sk_ref, q_ref,
    part, bc, bx, by, s1, s2, s3, spread, chunk, g1, g2, got, sends, arrivals, base, sketch
):
    ph = Phases(sends, arrivals)
    ph.greet(ph.peers())
    rank = om_ref.shape[2]
    quarter = x_ref.shape[1]
    for d in range(4):
        base[lax.rem(ph.other(d), 4)] = mm2r(x_ref[d], z_ref[d], NT).astype(BF16)
    weight = weight_ref[:, quarter_rows(ph.place, quarter)]
    mine = sketch.at[2 * lax.rem(ph.place, 2) + ph.place // 2]
    for pair in (0, 1):
        low, high = base[2 * pair], base[2 * pair + 1]
        both = mm(low, om_ref[0, :rank, :]) + mm(high, om_ref[0, rank:, :])
        mine[:, pair * rank : (pair + 1) * rank] = both.astype(BF16)
        put_halves(part, pair, mm2(jnp.transpose(low).astype(F32) * weight, high))
    low, high = mine[:, :rank], mine[:, rank:]
    put_halves(part, 2, mm2(jnp.transpose(low).astype(F32) * weight, high))
    ph.met(10)
    piece = quarter // 2

    def give_sketch(d, i):
        rows = mine.at[pl.ds(i * piece, piece), :]
        return ph.send(rows, rows, {"snap": ph.other(d)})

    def omega_products():
        for level in (0, 1):
            q_ref[level, 0] = mm2(zo_ref[level], om_ref[level, :rank, :], NT)
            q_ref[level, 1] = mm2r(om_ref[level, rank:, :], zo_ref[level], NT)

    bulk = [give_sketch(2, 0), give_sketch(1, 0)]
    sum_over_space(ph, part, bc, bx, by, s1, s2, s3, spread, omega_products)
    bulk += [give_sketch(2, 1), give_sketch(1, 1)]
    chunk[...] = (spread[0] + spread[1]) + (spread[2] + spread[3])
    give_over_space(ph, chunk, g1, g2, got)
    for d in range(3):
        out_ref[d] = whole(got, d)
    for copy in bulk:
        copy.wait_recv()
    for i, d in enumerate((0, 2, 1)):
        there = lax.rem(ph.other(d), 4)
        sk_ref[i] = sketch[2 * lax.rem(there, 2) + there // 2]
    ph.finish()


def sum_scratch(before, after, copies=29):
    return [
        pltpu.VMEM((2, before, 128, 128), F32),
        pltpu.VMEM((2, 3, before, 32, 128), F32),
        pltpu.VMEM((2, 3, before, 8, 128), F32),
        pltpu.VMEM((2, before, 128, 128), F32),
        pltpu.VMEM((2, before, 32, 128), F32),
        pltpu.VMEM((2, before, 8, 128), F32),
        pltpu.VMEM((4, 2, before, 8, 128), F32),
        pltpu.VMEM((2, after, 8, 128), F32),
        pltpu.VMEM((2, after, 32, 128), F32),
        pltpu.VMEM((2, after, 128, 128), F32),
        pltpu.VMEM((2, after, 256, 128), F32),
        pltpu.SemaphoreType.DMA((copies,)),
        pltpu.SemaphoreType.DMA((copies,)),
    ]


def near_identity(qa, cross, qb, a, t):
    t[...] = mm3(qa, mm3(cross, qb))
    a[...] = eye(cross.shape[0]) + t[...] + jnp.transpose(t[...])


def merge_factors(c_ref, om_ref, zo_ref, q_ref, out_ref, a, z, first, start, t, wide):
    rank = om_ref.shape[2]
    for pair in (0, 1):
        near_identity(q_ref[0, 0], c_ref[pair], q_ref[0, 1], a.at[pair], t.at[pair])
        z[pair] = zo_ref[0]
    factor(a, z, first, start, wide, 2, 3, 8)
    t[0] = mm3(q_ref[1, 0], z[0])
    t[1] = mm3(jnp.transpose(z[1]), q_ref[1, 1])
    near_identity(t[0], c_ref[2], t[1], a.at[2], t.at[0])
    z[2] = zo_ref[1]
    factor(a.at[pl.ds(2, 1)], z.at[pl.ds(2, 1)], first, start, wide, 1, 3, 8)
    last = z[2]
    for pair in (0, 1):
        u = mm2r(om_ref[1, pair * rank : (pair + 1) * rank, :], last, NT)
        out_ref[pair * rank : (pair + 1) * rank, :] = mm3(jnp.transpose(z[pair]), u)


def spread_kernel(
    rim_ref, sk_ref, mix_ref, base_ref, rims_ref, own, base, rim_out, rim_in, sends, arrivals
):
    ph = Phases(sends, arrivals)
    me, n = lax.axis_index("space"), lax.axis_size("space")
    near = ph.other(1)
    before, after = lax.rem(me + n - 1, n), lax.rem(me + 1, n)
    targets = [{"space": before}, {"space": after}]
    targets += [{"space": before, "snap": near}, {"space": after, "snap": near}]
    ph.greet([{"snap": near}] + targets)
    high, low = split(mix_ref[...])
    half = base.shape[0] // 2
    quarter = half // 2
    upper = lax.rem(ph.place, 2)
    second = ph.place // 2

    def rows_from(sk):
        found = (mm(sk, high) + mm(sk, low)).astype(BF16)
        return found.reshape(quarter, *own.shape[1:])

    own[pl.ds(second * quarter, quarter)] = rows_from(sk_ref[0])
    own[pl.ds((1 - second) * quarter, quarter)] = rows_from(sk_ref[1])
    ph.met(5)
    sent = upper * half + (1 - second) * quarter
    copy = ph.send(
        own.at[pl.ds((1 - second) * quarter, quarter)],
        base.at[pl.ds(sent, quarter)],
        {"snap": near},
    )
    for side in (0, 1):
        where = rim_ref[0, side] - upper * half
        block = own[jnp.clip(where, 0, half - 1)]
        inside = jnp.logical_and(where >= 0, where < half)
        rim_out[side] = jnp.where(inside, block, jnp.zeros_like(block))
    swaps = [
        ph.send(rim_out.at[0], rim_in.at[1, 0], targets[0]),
        ph.send(rim_out.at[1], rim_in.at[0, 0], targets[1]),
        ph.send(rim_out.at[0], rim_in.at[1, 1], targets[2]),
        ph.send(rim_out.at[1], rim_in.at[0, 1], targets[3]),
    ]
    base[pl.ds(upper * half, half)] = own[...]
    base[pl.ds((1 - upper) * half + second * quarter, quarter)] = rows_from(sk_ref[2])
    for swap in swaps:
        swap.wait_recv()
    rims_ref[:BLOCK, :] = jnp.where(me > 0, rim_in[0, 0] + rim_in[0, 1], 0)
    rims_ref[BLOCK:, :] = jnp.where(me < n - 1, rim_in[1, 0] + rim_in[1, 1], 0)
    copy.wait_recv()
    base_ref[...] = base[...].reshape(base_ref.shape)
    ph.finish()


def product_kernel(cols_ref, count_ref, full_ref, rims_ref, jac_ref, base_ref, out_ref, held):
    rows, rank = full_ref.shape
    blocks = rows // BLOCK
    base_ref[...] = full_ref[...]
    held[:rows, :] = full_ref[...]
    held[rows:, :] = rims_ref[...]
    count = count_ref[0]

    def block(b, _):
        here = pl.ds(pl.multiple_of(b * BLOCK, BLOCK), BLOCK)
        picked = [
            held[pl.ds(pl.multiple_of(cols_ref[b, k] * BLOCK, BLOCK), BLOCK), :] for k in range(NNZ)
        ]
        product = mm(jac_ref[here, :], jnp.concatenate(picked, axis=0))
        out_ref[here, :] = jnp.where(b < count, product, 0.0).astype(BF16)
        return 0

    lax.fori_loop(0, blocks, block, 0, unroll=2)


VM = pl.BlockSpec(memory_space=pltpu.VMEM)
SM = pl.BlockSpec(memory_space=pltpu.SMEM)
ANY = pl.BlockSpec(memory_space=pl.ANY)


def call(body, outs, ins, scratch, name, **params):
    return pl.pallas_call(
        body,
        out_shape=outs,
        in_specs=ins,
        out_specs=jax.tree.map(lambda _: VM, outs),
        scratch_shapes=scratch,
        compiler_params=pltpu.CompilerParams(vmem_limit_bytes=VMEM_LIMIT, **params),
        name=name,
    )


def on_device(snapshots, cell_volume, counts, rim_rows, jac_cols, jacobian, omega):
    rows, rank = snapshots.shape
    blocks, quarter = rows // BLOCK, rows // 4
    square = (rank, rank)
    wide = pltpu.VMEM((rank // 2, rank), F32)

    def squares(n):
        return pltpu.VMEM((n, rank, rank), F32)

    grams, parts, starts, weight = call(
        first_sum,
        [
            jax.ShapeDtypeStruct((4, rank, rank), F32),
            jax.ShapeDtypeStruct((4, quarter, rank), BF16),
            jax.ShapeDtypeStruct((2, rank, rank), F32),
            jax.ShapeDtypeStruct((1, rows), F32),
        ],
        [SM, ANY, VM, ANY],
        [pltpu.VMEM((2, 1, rank, rank // 2), F32)]
        + sum_scratch(1, 4, 33)
        + [
            pltpu.VMEM((rows, rank), BF16),
            pltpu.VMEM((2 * rank, rank), BF16),
            pltpu.SemaphoreType.DMA((2,)),
            pltpu.VMEM((rows, rank), BF16),
            pltpu.VMEM((3, quarter, rank), BF16),
            pltpu.VMEM(square, F32),
            squares(2),
            wide,
        ],
        "first_sum",
        collective_id=0,
        has_side_effects=True,
    )(counts, snapshots, cell_volume, omega)
    factors = call(
        gram_factors,
        jax.ShapeDtypeStruct((4, rank, rank), F32),
        [VM],
        [squares(4)] * 3 + [wide],
        "gram_factors",
    )(grams)
    cross, sketch, products = call(
        second_sum,
        [
            jax.ShapeDtypeStruct((3, rank, rank), F32),
            jax.ShapeDtypeStruct((3, quarter, 2 * rank), BF16),
            jax.ShapeDtypeStruct((2, 2, rank, rank), F32),
        ],
        [VM] * 5,
        [pltpu.VMEM((2, 3, rank, rank // 2), F32)]
        + sum_scratch(3, 3, 33)
        + [pltpu.VMEM((4, quarter, rank), BF16), pltpu.VMEM((4, quarter, 2 * rank), BF16)],
        "second_sum",
        collective_id=1,
        has_side_effects=True,
    )(factors, parts, weight, omega, starts)
    mix = call(
        merge_factors,
        jax.ShapeDtypeStruct((2 * rank, rank), F32),
        [VM] * 4,
        [squares(3), squares(3), squares(2), squares(2), squares(2), wide],
        "merge_factors",
    )(cross, omega, starts, products)
    full, rims = call(
        spread_kernel,
        [
            jax.ShapeDtypeStruct((rows, rank), BF16),
            jax.ShapeDtypeStruct((2 * BLOCK, rank), BF16),
        ],
        [SM, VM, VM],
        [
            pltpu.VMEM((blocks // 2, BLOCK, rank), BF16),
            pltpu.VMEM((blocks, BLOCK, rank), BF16),
            pltpu.VMEM((2, BLOCK, rank), BF16),
            pltpu.VMEM((2, 2, BLOCK, rank), BF16),
            pltpu.SemaphoreType.DMA((5,)),
            pltpu.SemaphoreType.DMA((5,)),
        ],
        "spread_rows",
        collective_id=2,
        has_side_effects=True,
    )(rim_rows, sketch, mix)
    basis, product = call(
        product_kernel,
        [jax.ShapeDtypeStruct((rows, rank), BF16)] * 2,
        [SM, SM, VM, VM, VM],
        [pltpu.VMEM((rows + 2 * BLOCK, rank), BF16)],
        "jac_product",
    )(jac_cols, counts, full, rims, jacobian)
    return (basis, product)


def solution(mesh):
    in_specs = (
        P("space", "snap"),
        P("space"),
        P("space"),
        P("space", None),
        P("space", None),
        P("space", None),
        P(),
    )
    out_specs = (P("space", "snap"), P("space", "snap"))
    return jax.shard_map(
        on_device, mesh=mesh, in_specs=in_specs, out_specs=out_specs, check_vma=False
    )
```

```python
import functools

import jax
import jax.numpy as jnp
from jax import lax
from jax.experimental import pallas as pl
from jax.experimental.pallas import tpu as pltpu
from jax.sharding import PartitionSpec as P

BLOCK = 64
NNZ = 8
LEVELS = 2
F32, BF16 = jnp.float32, jnp.bfloat16
NN = ((1,), (0,))
NT = ((1,), (1,))
TN = ((0,), (0,))
MESH = pl.DeviceIdType.MESH
VMEM_LIMIT = 48 * 1024 * 1024


def split(a):
    hi = a.astype(BF16)
    return hi, (a - hi.astype(F32)).astype(BF16)

def mm(a, b, dims=((1,), (0,))):
    return lax.dot_general(a, b, (dims, ((), ())), preferred_element_type=F32)


def mm3(a, b, dims=NN):
    ah, al = split(a)
    bh, bl = split(b)
    return mm(ah, bh, dims) + (mm(ah, bl, dims) + mm(al, bh, dims))

def leaf(aq, W=32):
    T = W // 8
    def panel(k, _):
        r0 = pl.multiple_of(k * W, W)
        rows = aq[pl.ds(r0, W), :]
        diag = pltpu.roll(rows[:, :128], lax.rem(128 - r0, 128), axis=1)
        C = [[jnp.broadcast_to(diag[8*t:8*t+8, m:m+1], (8, 128)) for t in range(T)] for m in range(W)]
        lane = lax.broadcasted_iota(jnp.int32, (8, 128), 1)
        sub = lax.broadcasted_iota(jnp.int32, (8, 128), 0)
        E = [(lane == sub + 8*t).astype(F32) for t in range(T)]
        scale = [jnp.zeros((8, 128), F32) for t in range(T)]
        for j in range(W):
            tj, sj = divmod(j, 8)
            piv = jnp.broadcast_to(C[j][tj][sj:sj+1, :], (8, 128))
            r = pl.reciprocal(piv, approx=True)
            f = [None]*T
            for t in range(tj, T):
                f[t] = C[j][t] * r
            f[tj] = jnp.where(sub > sj, f[tj], 0.0)
            for m in range(j + 1, W):
                tm, sm = divmod(m, 8)
                c = jnp.broadcast_to(C[j][tm][sm:sm+1, :], (8, 128))
                for t in range(tm, T):
                    C[m][t] = C[m][t] - f[t] * c
            e = jnp.broadcast_to(E[tj][sj:sj+1, :], (8, 128))
            for t in range(tj, T):
                E[t] = E[t] - f[t] * e
            scale[tj] = jnp.where(sub == sj, piv, scale[tj])
        E = [E[t] * lax.rsqrt(scale[t]) for t in range(T)]
        inv = jnp.concatenate(E, 0)[:, :W]
        R = mm3(inv, rows)
        low = jnp.transpose(R[:, :128])
        low = jnp.where(lax.broadcasted_iota(jnp.int32, low.shape, 0) >= r0 + W, low, 0.0)
        aq[...] = aq[...] - mm3(low, R)
        aq[pl.ds(r0, W), :] = R
        return 0
    lax.fori_loop(0, 128 // W, panel, 0)

def chol_upper(a, z, aq):
    ident = eye(128)
    aq[:, 128:] = ident
    aq[:, :128] = a[:128, :128]
    leaf(aq)
    z11 = aq[:, 128:]
    z[:128, :128] = z11
    l21 = mm3(a[128:, :128], z11, NT)
    aq[:, :128] = a[128:, 128:] - mm3(l21, l21, NT)
    aq[:, 128:] = ident
    z[128:, :128] = mm3(l21, z11)


def chol_lower(z, aq):
    leaf(aq)
    z22 = aq[:, 128:]
    z[128:, 128:] = z22
    z[128:, :128] = -mm3(z22, z[128:, :128])
    z[:128, 128:] = jnp.zeros((128, 128), F32)


def chol_inv(a, z, aq):
    chol_upper(a, z, aq)
    chol_lower(z, aq)


def iota(shape, dim):
    return lax.broadcasted_iota(jnp.int32, shape, dim)


def eye(n):
    return (iota((n, n), 0) == iota((n, n), 1)).astype(F32)


def mm3s(a, b, dims=NN):
    return mm(a[0], b[0], dims) + (mm(a[0], b[1], dims) + mm(a[1], b[0], dims))


def mm2(a, b, dims=NN):
    high, low = split(a)
    return mm(high, b, dims) + mm(low, b, dims)


def mm2r(a, b, dims=NN):
    high, low = split(b)
    return mm(a, high, dims) + mm(a, low, dims)


def newton_step(a_ref, z_ref, rough=False):
    a = a_ref[...]
    row, col = iota(a.shape, 0), iota(a.shape, 1)
    h = jnp.where(row > col, -a, jnp.where(row == col, 1.5 - 0.5 * a, 0.0))
    if rough:
        h = h.astype(BF16)
        t = mm2r(h, a)
        z = mm2r(h, z_ref[...])
        a_ref[...] = mm2(t, h, NT)
        z_ref[...] = z
        return
    h = split(h)
    t = mm3s(h, split(a))
    z = mm3s(h, split(z_ref[...]))
    a_ref[...] = mm3s(split(t), h, NT)
    z_ref[...] = z


def residual(a, count):
    worst = jnp.float32(0.0)
    for i in range(count):
        off = a[i] - eye(a.shape[1])
        total = jnp.sum(off * off)
        worst = jnp.maximum(worst, jnp.where(total < 1e30, total, 1e30))
    return worst


def factor(a, z, first, start, wide, count, fixed, most):
    for i in range(count):
        first[i] = a[i]
        start[i] = z[i]
    for step in range(fixed):
        for i in range(count):
            newton_step(a.at[i], z.at[i], step < 2)

    def unsettled(state):
        return jnp.logical_and(state[0] < most, state[1] > 3e-5)

    def again(state):
        for i in range(count):
            newton_step(a.at[i], z.at[i])
        return state[0] + 1, residual(a, count)

    left = lax.while_loop(unsettled, again, (jnp.int32(fixed), residual(a, count)))[1]

    @pl.when(left > 3e-5)
    def _():
        def direct(i, _):
            chol_inv(first.at[i], z.at[i], wide)
            z[i] = mm3(z[i], start[i])
            return 0

        lax.fori_loop(0, count, direct, 0)


class Phases:
    def __init__(self, sends, arrivals):
        self.sends, self.arrivals = sends, arrivals
        self.flying = []
        me = lax.axis_index("space")
        self.core = lax.rem(me, 2)
        self.y = lax.rem(me // 2, 4)
        self.x = me // 8
        self.snap = lax.axis_index("snap")
        self.place = lax.rem(self.snap, 4)
        self.used = 0

    def space(self, x, y, core):
        return (x * 4 + y) * 2 + core

    def peers(self):
        found = [{"space": self.space(self.x, self.y, 1 - self.core)}]
        for d in (1, 2, 3):
            found.append({"space": self.space(lax.rem(self.x + d, 4), self.y, self.core)})
            found.append({"space": self.space(self.x, lax.rem(self.y + d, 4), self.core)})
            found.append({"snap": self.other(d)})
        return found

    def other(self, d):
        place = self.place
        if d & 1:
            place = place + 1 - 2 * lax.rem(place, 2)
        if d & 2:
            place = place + 2 - 4 * (place // 2)
        return self.snap - self.place + place

    def send(self, src, dst, device):
        slot = self.used
        self.used += 1
        copy = pltpu.make_async_remote_copy(
            src_ref=src,
            dst_ref=dst,
            send_sem=self.sends.at[slot],
            recv_sem=self.arrivals.at[slot],
            device_id=device,
            device_id_type=MESH,
        )
        copy.start()
        self.flying.append(copy)
        return copy

    def finish(self):
        for copy in self.flying:
            copy.wait_send()

    def greet(self, devices):
        barrier = pltpu.get_barrier_semaphore()
        for device in devices:
            pl.semaphore_signal(barrier, inc=1, device_id=device, device_id_type=MESH)

    def met(self, count):
        pl.semaphore_wait(pltpu.get_barrier_semaphore(), count)

    def along(self, half, major, d):
        if (half == 0) == major:
            place = lax.rem(self.x + d, 4)
            return place, {"space": self.space(place, self.y, self.core)}
        place = lax.rem(self.y + d, 4)
        return place, {"space": self.space(self.x, place, self.core)}

    def own(self, half, major):
        return self.x if (half == 0) == major else self.y


def rows_of(place, size):
    return pl.ds(pl.multiple_of(place * size, size), size)


def sum_over_space(ph, part, bc, bx, by, s1, s2, s3, spread, makers, beside, after):
    twin = {"space": ph.space(ph.x, ph.y, 1 - ph.core)}
    copies = []
    for i, make in enumerate(makers):
        make()
        which = pl.ds(i, 1)
        copies.append(
            ph.send(part.at[:, which, rows_of(1 - ph.core, 128), :], bc.at[:, which], twin)
        )
    for copy in copies:
        copy.wait_recv()
    s1[...] = part[:, :, rows_of(ph.core, 128), :] + bc[...]
    copies = []
    for d in (1, 2, 3):
        for half in (0, 1):
            place, device = ph.along(half, True, d)
            copies.append(ph.send(s1.at[half, :, rows_of(place, 32), :], bx.at[half, d - 1], device))
    beside()
    for copy in copies:
        copy.wait_recv()
    for half in (0, 1):
        mine = s1[half, :, rows_of(ph.own(half, True), 32), :]
        s2[half] = mine + (bx[half, 0] + bx[half, 1] + bx[half, 2])
    copies = []
    for d in (1, 2, 3):
        for half in (0, 1):
            place, device = ph.along(half, False, d)
            copies.append(ph.send(s2.at[half, :, rows_of(place, 8), :], by.at[half, d - 1], device))
    for copy in copies:
        copy.wait_recv()
    for half in (0, 1):
        mine = s2[half, :, rows_of(ph.own(half, False), 8), :]
        s3[half] = mine + (by[half, 0] + by[half, 1] + by[half, 2])
    copies = []
    for d in (1, 2, 3):
        copies.append(ph.send(s3, spread.at[d], {"snap": ph.other(d)}))
    spread[0] = s3[...]
    after()
    for copy in copies:
        copy.wait_recv()


def give_over_space(ph, chunk, g1, out, beside=None):
    copies = []
    for half in (0, 1):
        mine = rows_of(ph.own(half, False), 8)
        for d in (1, 2, 3):
            _, device = ph.along(half, False, d)
            copies.append(ph.send(chunk.at[half], g1.at[half, :, mine, :], device))
        g1[half, :, mine, :] = chunk[half]
    for copy in copies:
        copy.wait_recv()
    twin = {"space": ph.space(ph.x, ph.y, 1 - ph.core)}
    copies, last = {}, []
    for d in (1, 3, 2):
        for half in (0, 1):
            mine = rows_of(ph.core * 4 + ph.own(half, True), 32)
            _, device = ph.along(half, True, d)
            copies[d, half] = ph.send(g1.at[half], out.at[half, :, mine, :], device)
    for half in (0, 1):
        mine = rows_of(ph.core * 4 + ph.own(half, True), 32)
        last.append(ph.send(g1.at[half], out.at[half, :, mine, :], twin))
        out[half, :, mine, :] = g1[half]
    if beside is not None:
        beside()
    for d in (1, 3, 2):
        for half in (0, 1):
            copies[d, half].wait_recv()
            origin = lax.rem(ph.own(half, True) + 4 - d, 4)
            theirs = out.at[half, :, rows_of(ph.core * 4 + origin, 32), :]
            last.append(ph.send(theirs, theirs, twin))
    for copy in last:
        copy.wait_recv()


def put_halves(ref, index, square):
    ref[0, index] = square[:, :128]
    ref[1, index] = square[:, 128:]


def whole(ref, index):
    return jnp.concatenate([ref[0, index], ref[1, index]], axis=1)


def quarter_rows(place, size):
    return rows_of(2 * lax.rem(place, 2) + place // 2, size)


def first_sum(
    count_ref, x_ref, volume_ref, om_ref, out_ref, parts_ref, zo_ref, weight_ref,
    part, bc, bx, by, s1, s2, s3, spread, chunk, g1, got, sends, arrivals,
    raw, om_local, volume_local, loads, local, parts, m, zo, wide
):
    ph = Phases(sends, arrivals)
    load = pltpu.make_async_copy(x_ref, raw, loads.at[0])
    load.start()
    om_load = pltpu.make_async_copy(om_ref.at[ph.core], om_local, loads.at[1])
    om_load.start()
    volume_load = pltpu.make_async_copy(volume_ref, volume_local, loads.at[2])
    volume_load.start()
    ph.greet(ph.peers())
    used = count_ref[0] * BLOCK
    rows = raw.shape[0]
    total = rows * lax.axis_size("space")
    volume_load.wait()
    volume = volume_local[...].reshape(1, rows)
    weight = jnp.where(iota((1, rows), 1) < used, volume, 0.0) / total
    weight_ref[...] = weight
    load.wait()
    local[...] = jnp.where(iota(raw.shape, 0) < used, raw[...], 0)
    weighted = jnp.transpose(local[...]).astype(F32) * weight
    put_halves(part, 0, mm2(weighted, local[...]))
    ph.met(10)
    quarter = parts.shape[1]

    def give_rows(d):
        there = ph.other(d)
        rows = quarter_rows(lax.rem(there, 4), quarter)
        return ph.send(local.at[rows, :], parts.at[d - 1], {"snap": there})

    bulk = [give_rows(2), give_rows(1)]
    om_load.wait()
    om = om_local[...]
    m[...] = mm(om, om, TN)
    mine = zo.at[ph.core]
    sum_over_space(
        ph, part, bc, bx, by, s1, s2, s3, spread,
        [lambda: None],
        lambda: chol_upper(m, mine, wide),
        lambda: bulk.append(give_rows(3)),
    )
    for d in range(4):
        chunk[:, d] = spread[d, :, 0]
    give_over_space(ph, chunk, g1, got, lambda: chol_lower(mine, wide))
    factor_copy = ph.send(mine, mine, {"space": ph.space(ph.x, ph.y, 1 - ph.core)})
    for d in range(4):
        out_ref[d] = whole(got, d)
    parts_ref[0] = local[quarter_rows(ph.place, quarter), :]
    for d, copy in zip((2, 1, 3), bulk):
        copy.wait_recv()
        parts_ref[d] = parts[d - 1]
    factor_copy.wait_recv()
    zo_ref[...] = zo[...]
    ph.finish()


def gram_factors(g_ref, z, a, first, start, wide):
    rank = g_ref.shape[1]
    diagonal = iota((rank, rank), 0) == iota((rank, rank), 1)
    for d in range(4):
        g = g_ref[d]
        pivots = jnp.where(diagonal, g, 0.0)
        down = lax.rsqrt(jnp.sum(pivots, axis=1, keepdims=True))
        across = lax.rsqrt(jnp.sum(pivots, axis=0, keepdims=True))
        a[d] = g * down * across
        z[d] = jnp.where(diagonal, down, 0.0)
    factor(a, z, first, start, wide, 4, 3, 8)


def second_sum(
    z_ref, x_ref, weight_ref, om_ref, zo_ref, out_ref, sk_ref, q_ref,
    part, bc, bx, by, s1, s2, s3, spread, chunk, g1, got, sends, arrivals, base, sketch
):
    ph = Phases(sends, arrivals)
    ph.greet(ph.peers())
    rank = om_ref.shape[2]
    quarter = x_ref.shape[1]
    for d in range(4):
        base[lax.rem(ph.other(d), 4)] = mm2r(x_ref[d], z_ref[d], NT).astype(BF16)
    weight = weight_ref[:, quarter_rows(ph.place, quarter)]
    mine = sketch.at[2 * lax.rem(ph.place, 2) + ph.place // 2]
    for pair in (0, 1):
        low, high = base[2 * pair], base[2 * pair + 1]
        both = mm(low, om_ref[0, :rank, :]) + mm(high, om_ref[0, rank:, :])
        mine[:, pair * rank : (pair + 1) * rank] = both.astype(BF16)

    def cross_gram(index, low, high):
        put_halves(part, index, mm2(jnp.transpose(low).astype(F32) * weight, high))

    makers = [
        lambda: cross_gram(0, base[0], base[1]),
        lambda: cross_gram(1, base[2], base[3]),
        lambda: cross_gram(2, mine[:, :rank], mine[:, rank:]),
    ]
    ph.met(10)
    piece = quarter // 2

    def give_sketch(d, i):
        rows = mine.at[pl.ds(i * piece, piece), :]
        return ph.send(rows, rows, {"snap": ph.other(d)})

    def omega_products():
        for level in (0, 1):
            q_ref[level, 0] = mm2(zo_ref[level], om_ref[level, :rank, :], NT)
            q_ref[level, 1] = mm2r(om_ref[level, rank:, :], zo_ref[level], NT)

    bulk = [give_sketch(2, 0), give_sketch(1, 0)]
    sum_over_space(
        ph, part, bc, bx, by, s1, s2, s3, spread,
        makers,
        omega_products,
        lambda: bulk.extend([give_sketch(2, 1), give_sketch(1, 1)]),
    )
    chunk[...] = (spread[0] + spread[1]) + (spread[2] + spread[3])
    give_over_space(ph, chunk, g1, got)
    for d in range(3):
        out_ref[d] = whole(got, d)
    for copy in bulk:
        copy.wait_recv()
    for i, d in enumerate((0, 2, 1)):
        there = lax.rem(ph.other(d), 4)
        sk_ref[i] = sketch[2 * lax.rem(there, 2) + there // 2]
    ph.finish()


def sum_scratch(before, after, copies):
    return [
        pltpu.VMEM((2, before, 128, 128), F32),
        pltpu.VMEM((2, 3, before, 32, 128), F32),
        pltpu.VMEM((2, 3, before, 8, 128), F32),
        pltpu.VMEM((2, before, 128, 128), F32),
        pltpu.VMEM((2, before, 32, 128), F32),
        pltpu.VMEM((2, before, 8, 128), F32),
        pltpu.VMEM((4, 2, before, 8, 128), F32),
        pltpu.VMEM((2, after, 8, 128), F32),
        pltpu.VMEM((2, after, 32, 128), F32),
        pltpu.VMEM((2, after, 256, 128), F32),
        pltpu.SemaphoreType.DMA((copies,)),
        pltpu.SemaphoreType.DMA((copies,)),
    ]


def near_identity(qa, cross, qb, a, t):
    t[...] = mm3(qa, mm3(cross, qb))
    a[...] = eye(cross.shape[0]) + t[...] + jnp.transpose(t[...])


def merge_factors(c_ref, om_ref, zo_ref, q_ref, out_ref, a, z, first, start, t, wide):
    rank = om_ref.shape[2]
    for pair in (0, 1):
        near_identity(q_ref[0, 0], c_ref[pair], q_ref[0, 1], a.at[pair], t.at[pair])
        z[pair] = zo_ref[0]
    factor(a, z, first, start, wide, 2, 3, 8)
    t[0] = mm3(q_ref[1, 0], z[0])
    t[1] = mm3(jnp.transpose(z[1]), q_ref[1, 1])
    near_identity(t[0], c_ref[2], t[1], a.at[2], t.at[0])
    z[2] = zo_ref[1]
    factor(a.at[pl.ds(2, 1)], z.at[pl.ds(2, 1)], first, start, wide, 1, 3, 8)
    last = z[2]
    for pair in (0, 1):
        u = mm2r(om_ref[1, pair * rank : (pair + 1) * rank, :], last, NT)
        out_ref[pair * rank : (pair + 1) * rank, :] = mm3(jnp.transpose(z[pair]), u)


def spread_kernel(
    rim_ref, sk_ref, mix_ref, out_ref, own, base, rim_out, rim_in, sends, arrivals
):
    ph = Phases(sends, arrivals)
    me, n = lax.axis_index("space"), lax.axis_size("space")
    near = ph.other(1)
    before, after = lax.rem(me + n - 1, n), lax.rem(me + 1, n)
    targets = [{"space": before}, {"space": after}]
    targets += [{"space": before, "snap": near}, {"space": after, "snap": near}]
    ph.greet([{"snap": near}] + targets)
    high, low = split(mix_ref[...])
    half = base.shape[0] // 2
    quarter = half // 2
    upper = lax.rem(ph.place, 2)
    second = ph.place // 2

    def rows_from(sk):
        found = (mm(sk, high) + mm(sk, low)).astype(BF16)
        return found.reshape(quarter, *own.shape[1:])

    own[pl.ds(second * quarter, quarter)] = rows_from(sk_ref[0])
    own[pl.ds((1 - second) * quarter, quarter)] = rows_from(sk_ref[1])
    ph.met(5)
    sent = upper * half + (1 - second) * quarter
    copy = ph.send(
        own.at[pl.ds((1 - second) * quarter, quarter)],
        base.at[pl.ds(sent, quarter)],
        {"snap": near},
    )
    for side in (0, 1):
        where = rim_ref[0, side] - upper * half
        block = own[jnp.clip(where, 0, half - 1)]
        inside = jnp.logical_and(where >= 0, where < half)
        rim_out[side] = jnp.where(inside, block, jnp.zeros_like(block))
    swaps = [
        ph.send(rim_out.at[0], rim_in.at[1, 0], targets[0]),
        ph.send(rim_out.at[1], rim_in.at[0, 0], targets[1]),
        ph.send(rim_out.at[0], rim_in.at[1, 1], targets[2]),
        ph.send(rim_out.at[1], rim_in.at[0, 1], targets[3]),
    ]
    base[pl.ds(upper * half, half)] = own[...]
    base[pl.ds((1 - upper) * half + second * quarter, quarter)] = rows_from(sk_ref[2])
    for swap in swaps:
        swap.wait_recv()
    blocks = base.shape[0]
    out_ref[blocks] = jnp.where(me > 0, rim_in[0, 0] + rim_in[0, 1], 0)
    out_ref[blocks + 1] = jnp.where(me < n - 1, rim_in[1, 0] + rim_in[1, 1], 0)
    copy.wait_recv()
    out_ref[:blocks] = base[...]
    ph.finish()


def product_kernel(cols_ref, count_ref, full_ref, jac_ref, base_ref, out_ref, product, sems):
    rank = full_ref.shape[2]
    blocks = jac_ref.shape[0] // BLOCK
    count = count_ref[0]
    copies = [pltpu.make_async_copy(full_ref.at[pl.ds(0, blocks)], base_ref, sems.at[0])]
    copies[0].start()
    pieces = 4
    size = blocks // pieces
    for piece in range(pieces):

        def block(i, _):
            b = piece * size + i
            picked = [full_ref[cols_ref[b, k]] for k in range(NNZ)]
            here = pl.ds(pl.multiple_of(b * BLOCK, BLOCK), BLOCK)
            found = mm(jac_ref[here, :], jnp.concatenate(picked, axis=0))
            product[b] = jnp.where(b < count, found, 0.0).astype(BF16)
            return 0

        lax.fori_loop(0, size, block, 0, unroll=3)
        done = pl.ds(piece * size, size)
        copies.append(
            pltpu.make_async_copy(product.at[done], out_ref.at[done], sems.at[piece + 1])
        )
        copies[-1].start()
    for copy in copies:
        copy.wait()


VM = pl.BlockSpec(memory_space=pltpu.VMEM)
SM = pl.BlockSpec(memory_space=pltpu.SMEM)
HBM = pl.BlockSpec(memory_space=pltpu.HBM)


def call(body, outs, ins, scratch, name, out=VM, limit=VMEM_LIMIT, **params):
    return pl.pallas_call(
        body,
        out_shape=outs,
        in_specs=ins,
        out_specs=jax.tree.map(lambda _: out, outs),
        scratch_shapes=scratch,
        compiler_params=pltpu.CompilerParams(vmem_limit_bytes=limit, **params),
        name=name,
    )


def on_device(snapshots, cell_volume, counts, rim_rows, jac_cols, jacobian, omega):
    rows, rank = snapshots.shape
    blocks, quarter = rows // BLOCK, rows // 4
    square = (rank, rank)
    wide = pltpu.VMEM((rank // 2, rank), F32)

    def squares(n):
        return pltpu.VMEM((n, rank, rank), F32)

    grams, parts, starts, weight = call(
        first_sum,
        [
            jax.ShapeDtypeStruct((4, rank, rank), F32),
            jax.ShapeDtypeStruct((4, quarter, rank), BF16),
            jax.ShapeDtypeStruct((2, rank, rank), F32),
            jax.ShapeDtypeStruct((1, rows), F32),
        ],
        [SM, HBM, HBM, HBM],
        [pltpu.VMEM((2, 1, rank, rank // 2), F32)]
        + sum_scratch(1, 4, 40)
        + [
            pltpu.VMEM((rows, rank), BF16),
            pltpu.VMEM((2 * rank, rank), BF16),
            pltpu.VMEM((rows,), F32),
            pltpu.SemaphoreType.DMA((3,)),
            pltpu.VMEM((rows, rank), BF16),
            pltpu.VMEM((3, quarter, rank), BF16),
            pltpu.VMEM(square, F32),
            squares(2),
            wide,
        ],
        "first_sum",
        limit=60 * 1024 * 1024,
        collective_id=0,
        has_side_effects=True,
    )(counts, snapshots, cell_volume, omega)
    factors = call(
        gram_factors,
        jax.ShapeDtypeStruct((4, rank, rank), F32),
        [VM],
        [squares(4)] * 3 + [wide],
        "gram_factors",
    )(grams)
    cross, sketch, products = call(
        second_sum,
        [
            jax.ShapeDtypeStruct((3, rank, rank), F32),
            jax.ShapeDtypeStruct((3, quarter, 2 * rank), BF16),
            jax.ShapeDtypeStruct((2, 2, rank, rank), F32),
        ],
        [VM] * 5,
        [pltpu.VMEM((2, 3, rank, rank // 2), F32)]
        + sum_scratch(3, 3, 42)
        + [pltpu.VMEM((4, quarter, rank), BF16), pltpu.VMEM((4, quarter, 2 * rank), BF16)],
        "second_sum",
        collective_id=1,
        has_side_effects=True,
    )(factors, parts, weight, omega, starts)
    mix = call(
        merge_factors,
        jax.ShapeDtypeStruct((2 * rank, rank), F32),
        [VM] * 4,
        [squares(3), squares(3), squares(2), squares(2), squares(2), wide],
        "merge_factors",
    )(cross, omega, starts, products)
    full = call(
        spread_kernel,
        jax.ShapeDtypeStruct((blocks + 2, BLOCK, rank), BF16),
        [SM, VM, VM],
        [
            pltpu.VMEM((blocks // 2, BLOCK, rank), BF16),
            pltpu.VMEM((blocks, BLOCK, rank), BF16),
            pltpu.VMEM((2, BLOCK, rank), BF16),
            pltpu.VMEM((2, 2, BLOCK, rank), BF16),
            pltpu.SemaphoreType.DMA((5,)),
            pltpu.SemaphoreType.DMA((5,)),
        ],
        "spread_rows",
        collective_id=2,
        has_side_effects=True,
    )(rim_rows, sketch, mix)
    basis, product = call(
        product_kernel,
        [jax.ShapeDtypeStruct((blocks, BLOCK, rank), BF16)] * 2,
        [SM, SM, VM, VM],
        [pltpu.VMEM((blocks, BLOCK, rank), BF16), pltpu.SemaphoreType.DMA((5,))],
        "jac_product",
        out=HBM,
    )(jac_cols, counts, full, jacobian)
    return (basis.reshape(rows, rank), product.reshape(rows, rank))


def solution(mesh):
    in_specs = (
        P("space", "snap"),
        P("space"),
        P("space"),
        P("space", None),
        P("space", None),
        P("space", None),
        P(),
    )
    out_specs = (P("space", "snap"), P("space", "snap"))
    return jax.shard_map(
        on_device, mesh=mesh, in_specs=in_specs, out_specs=out_specs, check_vma=False
    )
```

```python
import functools

import jax
import jax.numpy as jnp
from jax import lax
from jax.experimental import pallas as pl
from jax.experimental.pallas import tpu as pltpu
from jax.sharding import PartitionSpec as P

BLOCK = 64
NNZ = 8
LEVELS = 2
F32, BF16 = jnp.float32, jnp.bfloat16
NN = ((1,), (0,))
NT = ((1,), (1,))
TN = ((0,), (0,))
MESH = pl.DeviceIdType.MESH
VMEM_LIMIT = 48 * 1024 * 1024


def split(a):
    hi = a.astype(BF16)
    return hi, (a - hi.astype(F32)).astype(BF16)

def mm(a, b, dims=((1,), (0,))):
    return lax.dot_general(a, b, (dims, ((), ())), preferred_element_type=F32)


def mm3(a, b, dims=NN):
    ah, al = split(a)
    bh, bl = split(b)
    return mm(ah, bh, dims) + (mm(ah, bl, dims) + mm(al, bh, dims))

def leaf(aq, W=32):
    T = W // 8
    def panel(k, _):
        r0 = pl.multiple_of(k * W, W)
        rows = aq[pl.ds(r0, W), :]
        diag = pltpu.roll(rows[:, :128], lax.rem(128 - r0, 128), axis=1)
        C = [[jnp.broadcast_to(diag[8*t:8*t+8, m:m+1], (8, 128)) for t in range(T)] for m in range(W)]
        lane = lax.broadcasted_iota(jnp.int32, (8, 128), 1)
        sub = lax.broadcasted_iota(jnp.int32, (8, 128), 0)
        E = [(lane == sub + 8*t).astype(F32) for t in range(T)]
        scale = [jnp.zeros((8, 128), F32) for t in range(T)]
        for j in range(W):
            tj, sj = divmod(j, 8)
            piv = jnp.broadcast_to(C[j][tj][sj:sj+1, :], (8, 128))
            r = pl.reciprocal(piv, approx=True)
            f = [None]*T
            for t in range(tj, T):
                f[t] = C[j][t] * r
            f[tj] = jnp.where(sub > sj, f[tj], 0.0)
            for m in range(j + 1, W):
                tm, sm = divmod(m, 8)
                c = jnp.broadcast_to(C[j][tm][sm:sm+1, :], (8, 128))
                for t in range(tm, T):
                    C[m][t] = C[m][t] - f[t] * c
            e = jnp.broadcast_to(E[tj][sj:sj+1, :], (8, 128))
            for t in range(tj, T):
                E[t] = E[t] - f[t] * e
            scale[tj] = jnp.where(sub == sj, piv, scale[tj])
        E = [E[t] * lax.rsqrt(scale[t]) for t in range(T)]
        inv = jnp.concatenate(E, 0)[:, :W]
        R = mm3(inv, rows)
        low = jnp.transpose(R[:, :128])
        low = jnp.where(lax.broadcasted_iota(jnp.int32, low.shape, 0) >= r0 + W, low, 0.0)
        aq[...] = aq[...] - mm3(low, R)
        aq[pl.ds(r0, W), :] = R
        return 0
    lax.fori_loop(0, 128 // W, panel, 0)

def chol_upper(a, z, aq):
    ident = eye(128)
    aq[:, 128:] = ident
    aq[:, :128] = a[:128, :128]
    leaf(aq)
    z11 = aq[:, 128:]
    z[:128, :128] = z11
    l21 = mm3(a[128:, :128], z11, NT)
    aq[:, :128] = a[128:, 128:] - mm3(l21, l21, NT)
    aq[:, 128:] = ident
    z[128:, :128] = mm3(l21, z11)


def chol_lower(z, aq):
    leaf(aq)
    z22 = aq[:, 128:]
    z[128:, 128:] = z22
    z[128:, :128] = -mm3(z22, z[128:, :128])
    z[:128, 128:] = jnp.zeros((128, 128), F32)


def chol_inv(a, z, aq):
    chol_upper(a, z, aq)
    chol_lower(z, aq)


def iota(shape, dim):
    return lax.broadcasted_iota(jnp.int32, shape, dim)


def eye(n):
    return (iota((n, n), 0) == iota((n, n), 1)).astype(F32)


def mm3s(a, b, dims=NN):
    return mm(a[0], b[0], dims) + (mm(a[0], b[1], dims) + mm(a[1], b[0], dims))


def mm2(a, b, dims=NN):
    high, low = split(a)
    return mm(high, b, dims) + mm(low, b, dims)


def mm2r(a, b, dims=NN):
    high, low = split(b)
    return mm(a, high, dims) + mm(a, low, dims)


def newton_step(a_ref, z_ref, rough=False):
    a = a_ref[...]
    row, col = iota(a.shape, 0), iota(a.shape, 1)
    h = jnp.where(row > col, -a, jnp.where(row == col, 1.5 - 0.5 * a, 0.0))
    if rough:
        h = h.astype(BF16)
        t = mm2r(h, a)
        z = mm2r(h, z_ref[...])
        a_ref[...] = mm2(t, h, NT)
        z_ref[...] = z
        return
    h = split(h)
    t = mm3s(h, split(a))
    z = mm3s(h, split(z_ref[...]))
    a_ref[...] = mm3s(split(t), h, NT)
    z_ref[...] = z


def residual(a, count):
    worst = jnp.float32(0.0)
    for i in range(count):
        off = a[i] - eye(a.shape[1])
        total = jnp.sum(off * off)
        worst = jnp.maximum(worst, jnp.where(total < 1e30, total, 1e30))
    return worst


def factor(a, z, first, start, wide, count, fixed, most):
    for i in range(count):
        first[i] = a[i]
        start[i] = z[i]
    for step in range(fixed):
        for i in range(count):
            newton_step(a.at[i], z.at[i], step < 2)

    def unsettled(state):
        return jnp.logical_and(state[0] < most, state[1] > 3e-5)

    def again(state):
        for i in range(count):
            newton_step(a.at[i], z.at[i])
        return state[0] + 1, residual(a, count)

    left = lax.while_loop(unsettled, again, (jnp.int32(fixed), residual(a, count)))[1]

    @pl.when(left > 3e-5)
    def _():
        def direct(i, _):
            chol_inv(first.at[i], z.at[i], wide)
            z[i] = mm3(z[i], start[i])
            return 0

        lax.fori_loop(0, count, direct, 0)


class Phases:
    def __init__(self, sends, arrivals):
        self.sends, self.arrivals = sends, arrivals
        self.flying = []
        me = lax.axis_index("space")
        self.core = lax.rem(me, 2)
        self.y = lax.rem(me // 2, 4)
        self.x = me // 8
        self.snap = lax.axis_index("snap")
        self.place = lax.rem(self.snap, 4)
        self.used = 0

    def space(self, x, y, core):
        return (x * 4 + y) * 2 + core

    def peers(self):
        found = [{"space": self.space(self.x, self.y, 1 - self.core)}]
        for d in (1, 2, 3):
            found.append({"space": self.space(lax.rem(self.x + d, 4), self.y, self.core)})
            found.append({"space": self.space(self.x, lax.rem(self.y + d, 4), self.core)})
            found.append({"snap": self.other(d)})
        return found

    def other(self, d):
        place = self.place
        if d & 1:
            place = place + 1 - 2 * lax.rem(place, 2)
        if d & 2:
            place = place + 2 - 4 * (place // 2)
        return self.snap - self.place + place

    def send(self, src, dst, device):
        slot = self.used
        self.used += 1
        copy = pltpu.make_async_remote_copy(
            src_ref=src,
            dst_ref=dst,
            send_sem=self.sends.at[slot],
            recv_sem=self.arrivals.at[slot],
            device_id=device,
            device_id_type=MESH,
        )
        copy.start()
        self.flying.append(copy)
        return copy

    def finish(self):
        for copy in self.flying:
            copy.wait_send()

    def greet(self, devices):
        barrier = pltpu.get_barrier_semaphore()
        for device in devices:
            pl.semaphore_signal(barrier, inc=1, device_id=device, device_id_type=MESH)

    def met(self, count):
        pl.semaphore_wait(pltpu.get_barrier_semaphore(), count)

    def along(self, half, major, d):
        if (half == 0) == major:
            place = lax.rem(self.x + d, 4)
            return place, {"space": self.space(place, self.y, self.core)}
        place = lax.rem(self.y + d, 4)
        return place, {"space": self.space(self.x, place, self.core)}

    def own(self, half, major):
        return self.x if (half == 0) == major else self.y


def rows_of(place, size):
    return pl.ds(pl.multiple_of(place * size, size), size)


def sum_over_space(ph, part, bc, bx, by, s1, s2, s3, spread, makers, beside, after):
    twin = {"space": ph.space(ph.x, ph.y, 1 - ph.core)}
    copies = []
    for i, make in enumerate(makers):
        make()
        which = pl.ds(i, 1)
        copies.append(
            ph.send(part.at[:, which, rows_of(1 - ph.core, 128), :], bc.at[:, which], twin)
        )
    for copy in copies:
        copy.wait_recv()
    s1[...] = part[:, :, rows_of(ph.core, 128), :] + bc[...]
    copies = []
    for d in (1, 2, 3):
        for half in (0, 1):
            place, device = ph.along(half, True, d)
            copies.append(ph.send(s1.at[half, :, rows_of(place, 32), :], bx.at[half, d - 1], device))
    beside()
    for copy in copies:
        copy.wait_recv()
    for half in (0, 1):
        mine = s1[half, :, rows_of(ph.own(half, True), 32), :]
        s2[half] = mine + (bx[half, 0] + bx[half, 1] + bx[half, 2])
    copies = []
    for d in (1, 2, 3):
        for half in (0, 1):
            place, device = ph.along(half, False, d)
            copies.append(ph.send(s2.at[half, :, rows_of(place, 8), :], by.at[half, d - 1], device))
    for copy in copies:
        copy.wait_recv()
    for half in (0, 1):
        mine = s2[half, :, rows_of(ph.own(half, False), 8), :]
        s3[half] = mine + (by[half, 0] + by[half, 1] + by[half, 2])
    copies = []
    for d in (1, 2, 3):
        copies.append(ph.send(s3, spread.at[d], {"snap": ph.other(d)}))
    spread[0] = s3[...]
    for copy in copies:
        copy.wait_recv()
    after()


def give_over_space(ph, chunk, g1, out, beside=None):
    copies = []
    for half in (0, 1):
        mine = rows_of(ph.own(half, False), 8)
        for d in (1, 2, 3):
            _, device = ph.along(half, False, d)
            copies.append(ph.send(chunk.at[half], g1.at[half, :, mine, :], device))
        g1[half, :, mine, :] = chunk[half]
    for copy in copies:
        copy.wait_recv()
    twin = {"space": ph.space(ph.x, ph.y, 1 - ph.core)}
    copies, last = {}, []
    for d in (1, 3, 2):
        for half in (0, 1):
            mine = rows_of(ph.core * 4 + ph.own(half, True), 32)
            _, device = ph.along(half, True, d)
            copies[d, half] = ph.send(g1.at[half], out.at[half, :, mine, :], device)
    for half in (0, 1):
        mine = rows_of(ph.core * 4 + ph.own(half, True), 32)
        last.append(ph.send(g1.at[half], out.at[half, :, mine, :], twin))
        out[half, :, mine, :] = g1[half]
    if beside is not None:
        beside()
    for d in (1, 3, 2):
        for half in (0, 1):
            copies[d, half].wait_recv()
            origin = lax.rem(ph.own(half, True) + 4 - d, 4)
            theirs = out.at[half, :, rows_of(ph.core * 4 + origin, 32), :]
            last.append(ph.send(theirs, theirs, twin))
    for copy in last:
        copy.wait_recv()


def put_halves(ref, index, square):
    ref[0, index] = square[:, :128]
    ref[1, index] = square[:, 128:]


def whole(ref, index):
    return jnp.concatenate([ref[0, index], ref[1, index]], axis=1)


def quarter_rows(place, size):
    return rows_of(2 * lax.rem(place, 2) + place // 2, size)


def first_sum(
    count_ref, x_ref, volume_ref, om_ref, out_ref, parts_ref, zo_ref, weight_ref,
    part, bc, bx, by, s1, s2, s3, spread, chunk, g1, got, sends, arrivals,
    raw, om_local, volume_local, loads, local, parts, m, zo, wide
):
    ph = Phases(sends, arrivals)
    load = pltpu.make_async_copy(x_ref, raw, loads.at[0])
    load.start()
    om_load = pltpu.make_async_copy(om_ref.at[ph.core], om_local, loads.at[1])
    om_load.start()
    volume_load = pltpu.make_async_copy(volume_ref, volume_local, loads.at[2])
    volume_load.start()
    ph.greet(ph.peers())
    used = count_ref[0] * BLOCK
    rows = raw.shape[0]
    total = rows * lax.axis_size("space")
    volume_load.wait()
    volume = volume_local[...].reshape(1, rows)
    weight = jnp.where(iota((1, rows), 1) < used, volume, 0.0) / total
    weight_ref[...] = weight
    load.wait()
    local[...] = jnp.where(iota(raw.shape, 0) < used, raw[...], 0)
    weighted = jnp.transpose(local[...]).astype(F32) * weight
    put_halves(part, 0, mm2(weighted, local[...]))
    ph.met(10)
    quarter = parts.shape[1]

    def give_rows(d):
        there = ph.other(d)
        rows = quarter_rows(lax.rem(there, 4), quarter)
        return ph.send(local.at[rows, :], parts.at[d - 1], {"snap": there})

    bulk = [give_rows(2), give_rows(1)]
    om_load.wait()
    om = om_local[...]
    m[...] = mm(om, om, TN)
    mine = zo.at[ph.core]
    sum_over_space(
        ph, part, bc, bx, by, s1, s2, s3, spread,
        [lambda: None],
        lambda: chol_upper(m, mine, wide),
        lambda: bulk.append(give_rows(3)),
    )
    for d in range(4):
        chunk[:, d] = spread[d, :, 0]
    give_over_space(ph, chunk, g1, got, lambda: chol_lower(mine, wide))
    factor_copy = ph.send(mine, mine, {"space": ph.space(ph.x, ph.y, 1 - ph.core)})
    for d in range(4):
        out_ref[d] = whole(got, d)
    parts_ref[0] = local[quarter_rows(ph.place, quarter), :]
    for d, copy in zip((2, 1, 3), bulk):
        copy.wait_recv()
        parts_ref[d] = parts[d - 1]
    factor_copy.wait_recv()
    zo_ref[...] = zo[...]
    ph.finish()


def gram_factors(g_ref, z, a, first, start, wide):
    rank = g_ref.shape[1]
    diagonal = iota((rank, rank), 0) == iota((rank, rank), 1)
    for d in range(4):
        g = g_ref[d]
        pivots = jnp.where(diagonal, g, 0.0)
        down = lax.rsqrt(jnp.sum(pivots, axis=1, keepdims=True))
        across = lax.rsqrt(jnp.sum(pivots, axis=0, keepdims=True))
        a[d] = g * down * across
        z[d] = jnp.where(diagonal, down, 0.0)
    factor(a, z, first, start, wide, 4, 3, 8)


def second_sum(
    z_ref, x_ref, weight_ref, om_ref, zo_ref, out_ref, sk_ref, q_ref,
    part, bc, bx, by, s1, s2, s3, spread, chunk, g1, got, sends, arrivals, base, sketch
):
    ph = Phases(sends, arrivals)
    ph.greet(ph.peers())
    rank = om_ref.shape[2]
    quarter = x_ref.shape[1]
    for d in range(4):
        base[lax.rem(ph.other(d), 4)] = mm2r(x_ref[d], z_ref[d], NT).astype(BF16)
    weight = weight_ref[:, quarter_rows(ph.place, quarter)]
    mine = sketch.at[2 * lax.rem(ph.place, 2) + ph.place // 2]
    for pair in (0, 1):
        low, high = base[2 * pair], base[2 * pair + 1]
        both = mm(low, om_ref[0, :rank, :]) + mm(high, om_ref[0, rank:, :])
        mine[:, pair * rank : (pair + 1) * rank] = both.astype(BF16)

    def cross_gram(index, low, high):
        put_halves(part, index, mm2(jnp.transpose(low).astype(F32) * weight, high))

    makers = [
        lambda: cross_gram(0, base[0], base[1]),
        lambda: cross_gram(1, base[2], base[3]),
        lambda: cross_gram(2, mine[:, :rank], mine[:, rank:]),
    ]
    ph.met(10)
    piece = quarter // 2

    def give_sketch(d, i):
        rows = mine.at[pl.ds(i * piece, piece), :]
        return ph.send(rows, rows, {"snap": ph.other(d)})

    def omega_products():
        for level in (0, 1):
            q_ref[level, 0] = mm2(zo_ref[level], om_ref[level, :rank, :], NT)
            q_ref[level, 1] = mm2r(om_ref[level, rank:, :], zo_ref[level], NT)

    bulk = [give_sketch(2, 0), give_sketch(1, 0)]
    sum_over_space(
        ph, part, bc, bx, by, s1, s2, s3, spread,
        makers,
        omega_products,
        lambda: bulk.extend([give_sketch(2, 1), give_sketch(1, 1)]),
    )
    chunk[...] = (spread[0] + spread[1]) + (spread[2] + spread[3])
    give_over_space(ph, chunk, g1, got)
    for d in range(3):
        out_ref[d] = whole(got, d)
    for copy in bulk:
        copy.wait_recv()
    for i, d in enumerate((0, 2, 1)):
        there = lax.rem(ph.other(d), 4)
        sk_ref[i] = sketch[2 * lax.rem(there, 2) + there // 2]
    ph.finish()


def sum_scratch(before, after, copies):
    return [
        pltpu.VMEM((2, before, 128, 128), F32),
        pltpu.VMEM((2, 3, before, 32, 128), F32),
        pltpu.VMEM((2, 3, before, 8, 128), F32),
        pltpu.VMEM((2, before, 128, 128), F32),
        pltpu.VMEM((2, before, 32, 128), F32),
        pltpu.VMEM((2, before, 8, 128), F32),
        pltpu.VMEM((4, 2, before, 8, 128), F32),
        pltpu.VMEM((2, after, 8, 128), F32),
        pltpu.VMEM((2, after, 32, 128), F32),
        pltpu.VMEM((2, after, 256, 128), F32),
        pltpu.SemaphoreType.DMA((copies,)),
        pltpu.SemaphoreType.DMA((copies,)),
    ]


def near_identity(qa, cross, qb, a, t):
    t[...] = mm3(qa, mm3(cross, qb))
    a[...] = eye(cross.shape[0]) + t[...] + jnp.transpose(t[...])


def merge_factors(c_ref, zo_ref, q_ref, z, a, first, start, t, wide):
    for pair in (0, 1):
        near_identity(q_ref[0, 0], c_ref[pair], q_ref[0, 1], a.at[pair], t.at[pair])
        z[pair] = zo_ref[0]
    factor(a, z, first, start, wide, 2, 3, 8)
    t[0] = mm3(q_ref[1, 0], z[0])
    t[1] = mm3(jnp.transpose(z[1]), q_ref[1, 1])
    near_identity(t[0], c_ref[2], t[1], a.at[2], t.at[0])
    z[2] = zo_ref[1]
    factor(a.at[pl.ds(2, 1)], z.at[pl.ds(2, 1)], first, start, wide, 1, 3, 8)


def spread_kernel(
    rim_ref, sk_ref, z_ref, om_ref, out_ref, own, base, rim_out, rim_in, sends, arrivals
):
    ph = Phases(sends, arrivals)
    me, n = lax.axis_index("space"), lax.axis_size("space")
    near = ph.other(1)
    before, after = lax.rem(me + n - 1, n), lax.rem(me + 1, n)
    targets = [{"space": before}, {"space": after}]
    targets += [{"space": before, "snap": near}, {"space": after, "snap": near}]
    ph.greet([{"snap": near}] + targets)
    rank = om_ref.shape[2]
    mix = []
    for pair in (0, 1):
        u = mm2r(om_ref[1, pair * rank : (pair + 1) * rank, :], z_ref[2], NT)
        mix.append(mm3(jnp.transpose(z_ref[pair]), u))
    high, low = split(jnp.concatenate(mix, axis=0))
    half = base.shape[0] // 2
    quarter = half // 2
    upper = lax.rem(ph.place, 2)
    second = ph.place // 2

    def rows_from(sk):
        found = (mm(sk, high) + mm(sk, low)).astype(BF16)
        return found.reshape(quarter, *own.shape[1:])

    own[pl.ds(second * quarter, quarter)] = rows_from(sk_ref[0])
    own[pl.ds((1 - second) * quarter, quarter)] = rows_from(sk_ref[1])
    ph.met(5)
    sent = upper * half + (1 - second) * quarter
    copy = ph.send(
        own.at[pl.ds((1 - second) * quarter, quarter)],
        base.at[pl.ds(sent, quarter)],
        {"snap": near},
    )
    for side in (0, 1):
        where = rim_ref[0, side] - upper * half
        block = own[jnp.clip(where, 0, half - 1)]
        inside = jnp.logical_and(where >= 0, where < half)
        rim_out[side] = jnp.where(inside, block, jnp.zeros_like(block))
    swaps = [
        ph.send(rim_out.at[0], rim_in.at[1, 0], targets[0]),
        ph.send(rim_out.at[1], rim_in.at[0, 0], targets[1]),
        ph.send(rim_out.at[0], rim_in.at[1, 1], targets[2]),
        ph.send(rim_out.at[1], rim_in.at[0, 1], targets[3]),
    ]
    base[pl.ds(upper * half, half)] = own[...]
    base[pl.ds((1 - upper) * half + second * quarter, quarter)] = rows_from(sk_ref[2])
    for swap in swaps:
        swap.wait_recv()
    blocks = base.shape[0]
    out_ref[blocks] = jnp.where(me > 0, rim_in[0, 0] + rim_in[0, 1], 0)
    out_ref[blocks + 1] = jnp.where(me < n - 1, rim_in[1, 0] + rim_in[1, 1], 0)
    copy.wait_recv()
    out_ref[:blocks] = base[...]
    ph.finish()


def product_kernel(cols_ref, count_ref, full_ref, jac_ref, base_ref, out_ref, product, sems):
    rank = full_ref.shape[2]
    blocks = jac_ref.shape[0] // BLOCK
    count = count_ref[0]
    copies = [pltpu.make_async_copy(full_ref.at[pl.ds(0, blocks)], base_ref, sems.at[0])]
    copies[0].start()
    pieces = 4
    size = blocks // pieces
    for piece in range(pieces):

        def block(i, _):
            b = piece * size + i
            picked = [full_ref[cols_ref[b, k]] for k in range(NNZ)]
            here = pl.ds(pl.multiple_of(b * BLOCK, BLOCK), BLOCK)
            found = mm(jac_ref[here, :], jnp.concatenate(picked, axis=0))
            product[b] = jnp.where(b < count, found, 0.0).astype(BF16)
            return 0

        lax.fori_loop(0, size, block, 0, unroll=3)
        done = pl.ds(piece * size, size)
        copies.append(
            pltpu.make_async_copy(product.at[done], out_ref.at[done], sems.at[piece + 1])
        )
        copies[-1].start()
    for copy in copies:
        copy.wait()


VM = pl.BlockSpec(memory_space=pltpu.VMEM)
SM = pl.BlockSpec(memory_space=pltpu.SMEM)
HBM = pl.BlockSpec(memory_space=pltpu.HBM)


def call(body, outs, ins, scratch, name, out=VM, limit=VMEM_LIMIT, **params):
    return pl.pallas_call(
        body,
        out_shape=outs,
        in_specs=ins,
        out_specs=jax.tree.map(lambda _: out, outs),
        scratch_shapes=scratch,
        compiler_params=pltpu.CompilerParams(vmem_limit_bytes=limit, **params),
        name=name,
    )


def on_device(snapshots, cell_volume, counts, rim_rows, jac_cols, jacobian, omega):
    rows, rank = snapshots.shape
    blocks, quarter = rows // BLOCK, rows // 4
    square = (rank, rank)
    wide = pltpu.VMEM((rank // 2, rank), F32)

    def squares(n):
        return pltpu.VMEM((n, rank, rank), F32)

    grams, parts, starts, weight = call(
        first_sum,
        [
            jax.ShapeDtypeStruct((4, rank, rank), F32),
            jax.ShapeDtypeStruct((4, quarter, rank), BF16),
            jax.ShapeDtypeStruct((2, rank, rank), F32),
            jax.ShapeDtypeStruct((1, rows), F32),
        ],
        [SM, HBM, HBM, HBM],
        [pltpu.VMEM((2, 1, rank, rank // 2), F32)]
        + sum_scratch(1, 4, 40)
        + [
            pltpu.VMEM((rows, rank), BF16),
            pltpu.VMEM((2 * rank, rank), BF16),
            pltpu.VMEM((rows,), F32),
            pltpu.SemaphoreType.DMA((3,)),
            pltpu.VMEM((rows, rank), BF16),
            pltpu.VMEM((3, quarter, rank), BF16),
            pltpu.VMEM(square, F32),
            squares(2),
            wide,
        ],
        "first_sum",
        limit=60 * 1024 * 1024,
        collective_id=0,
        has_side_effects=True,
    )(counts, snapshots, cell_volume, omega)
    factors = call(
        gram_factors,
        jax.ShapeDtypeStruct((4, rank, rank), F32),
        [VM],
        [squares(4)] * 3 + [wide],
        "gram_factors",
    )(grams)
    cross, sketch, products = call(
        second_sum,
        [
            jax.ShapeDtypeStruct((3, rank, rank), F32),
            jax.ShapeDtypeStruct((3, quarter, 2 * rank), BF16),
            jax.ShapeDtypeStruct((2, 2, rank, rank), F32),
        ],
        [VM] * 5,
        [pltpu.VMEM((2, 3, rank, rank // 2), F32)]
        + sum_scratch(3, 3, 42)
        + [pltpu.VMEM((4, quarter, rank), BF16), pltpu.VMEM((4, quarter, 2 * rank), BF16)],
        "second_sum",
        collective_id=1,
        has_side_effects=True,
    )(factors, parts, weight, omega, starts)
    merged = call(
        merge_factors,
        jax.ShapeDtypeStruct((3, rank, rank), F32),
        [VM] * 3,
        [squares(3), squares(2), squares(2), squares(2), wide],
        "merge_factors",
    )(cross, starts, products)
    full = call(
        spread_kernel,
        jax.ShapeDtypeStruct((blocks + 2, BLOCK, rank), BF16),
        [SM, VM, VM, VM],
        [
            pltpu.VMEM((blocks // 2, BLOCK, rank), BF16),
            pltpu.VMEM((blocks, BLOCK, rank), BF16),
            pltpu.VMEM((2, BLOCK, rank), BF16),
            pltpu.VMEM((2, 2, BLOCK, rank), BF16),
            pltpu.SemaphoreType.DMA((5,)),
            pltpu.SemaphoreType.DMA((5,)),
        ],
        "spread_rows",
        collective_id=2,
        has_side_effects=True,
    )(rim_rows, sketch, merged, omega)
    basis, product = call(
        product_kernel,
        [jax.ShapeDtypeStruct((blocks, BLOCK, rank), BF16)] * 2,
        [SM, SM, VM, VM],
        [pltpu.VMEM((blocks, BLOCK, rank), BF16), pltpu.SemaphoreType.DMA((5,))],
        "jac_product",
        out=HBM,
    )(jac_cols, counts, full, jacobian)
    return (basis.reshape(rows, rank), product.reshape(rows, rank))


def solution(mesh):
    in_specs = (
        P("space", "snap"),
        P("space"),
        P("space"),
        P("space", None),
        P("space", None),
        P("space", None),
        P(),
    )
    out_specs = (P("space", "snap"), P("space", "snap"))
    return jax.shard_map(
        on_device, mesh=mesh, in_specs=in_specs, out_specs=out_specs, check_vma=False
    )
```

```python
import functools

import jax
import jax.numpy as jnp
from jax import lax
from jax.experimental import pallas as pl
from jax.experimental.pallas import tpu as pltpu
from jax.sharding import PartitionSpec as P

BLOCK = 64
NNZ = 8
LEVELS = 2
F32, BF16 = jnp.float32, jnp.bfloat16
NN = ((1,), (0,))
NT = ((1,), (1,))
TN = ((0,), (0,))
MESH = pl.DeviceIdType.MESH
VMEM_LIMIT = 48 * 1024 * 1024


def split(a):
    hi = a.astype(BF16)
    return hi, (a - hi.astype(F32)).astype(BF16)

def mm(a, b, dims=((1,), (0,))):
    return lax.dot_general(a, b, (dims, ((), ())), preferred_element_type=F32)


def mm3(a, b, dims=NN):
    ah, al = split(a)
    bh, bl = split(b)
    return mm(ah, bh, dims) + (mm(ah, bl, dims) + mm(al, bh, dims))

def leaf(aq, W=32):
    T = W // 8
    def panel(k, _):
        r0 = pl.multiple_of(k * W, W)
        rows = aq[pl.ds(r0, W), :]
        diag = pltpu.roll(rows[:, :128], lax.rem(128 - r0, 128), axis=1)
        C = [[jnp.broadcast_to(diag[8*t:8*t+8, m:m+1], (8, 128)) for t in range(T)] for m in range(W)]
        lane = lax.broadcasted_iota(jnp.int32, (8, 128), 1)
        sub = lax.broadcasted_iota(jnp.int32, (8, 128), 0)
        E = [(lane == sub + 8*t).astype(F32) for t in range(T)]
        scale = [jnp.zeros((8, 128), F32) for t in range(T)]
        for j in range(W):
            tj, sj = divmod(j, 8)
            piv = jnp.broadcast_to(C[j][tj][sj:sj+1, :], (8, 128))
            r = pl.reciprocal(piv, approx=True)
            f = [None]*T
            for t in range(tj, T):
                f[t] = C[j][t] * r
            f[tj] = jnp.where(sub > sj, f[tj], 0.0)
            for m in range(j + 1, W):
                tm, sm = divmod(m, 8)
                c = jnp.broadcast_to(C[j][tm][sm:sm+1, :], (8, 128))
                for t in range(tm, T):
                    C[m][t] = C[m][t] - f[t] * c
            e = jnp.broadcast_to(E[tj][sj:sj+1, :], (8, 128))
            for t in range(tj, T):
                E[t] = E[t] - f[t] * e
            scale[tj] = jnp.where(sub == sj, piv, scale[tj])
        E = [E[t] * lax.rsqrt(scale[t]) for t in range(T)]
        inv = jnp.concatenate(E, 0)[:, :W]
        R = mm3(inv, rows)
        low = jnp.transpose(R[:, :128])
        low = jnp.where(lax.broadcasted_iota(jnp.int32, low.shape, 0) >= r0 + W, low, 0.0)
        aq[...] = aq[...] - mm3(low, R)
        aq[pl.ds(r0, W), :] = R
        return 0
    lax.fori_loop(0, 128 // W, panel, 0)

def chol_upper(a, z, aq):
    ident = eye(128)
    aq[:, 128:] = ident
    aq[:, :128] = a[:128, :128]
    leaf(aq)
    z11 = aq[:, 128:]
    z[:128, :128] = z11
    l21 = mm3(a[128:, :128], z11, NT)
    aq[:, :128] = a[128:, 128:] - mm3(l21, l21, NT)
    aq[:, 128:] = ident
    z[128:, :128] = mm3(l21, z11)


def chol_lower(z, aq):
    leaf(aq)
    z22 = aq[:, 128:]
    z[128:, 128:] = z22
    z[128:, :128] = -mm3(z22, z[128:, :128])
    z[:128, 128:] = jnp.zeros((128, 128), F32)


def chol_inv(a, z, aq):
    chol_upper(a, z, aq)
    chol_lower(z, aq)


def iota(shape, dim):
    return lax.broadcasted_iota(jnp.int32, shape, dim)


def eye(n):
    return (iota((n, n), 0) == iota((n, n), 1)).astype(F32)


def mm3s(a, b, dims=NN):
    return mm(a[0], b[0], dims) + (mm(a[0], b[1], dims) + mm(a[1], b[0], dims))


def mm2(a, b, dims=NN):
    high, low = split(a)
    return mm(high, b, dims) + mm(low, b, dims)


def mm2r(a, b, dims=NN):
    high, low = split(b)
    return mm(a, high, dims) + mm(a, low, dims)


def newton_step(a_ref, z_ref, rough=False):
    a = a_ref[...]
    row, col = iota(a.shape, 0), iota(a.shape, 1)
    h = jnp.where(row > col, -a, jnp.where(row == col, 1.5 - 0.5 * a, 0.0))
    if rough:
        h = h.astype(BF16)
        t = mm2r(h, a)
        z = mm2r(h, z_ref[...])
        a_ref[...] = mm2(t, h, NT)
        z_ref[...] = z
        return
    h = split(h)
    t = mm3s(h, split(a))
    z = mm3s(h, split(z_ref[...]))
    a_ref[...] = mm3s(split(t), h, NT)
    z_ref[...] = z


def residual(a, count):
    worst = jnp.float32(0.0)
    for i in range(count):
        off = a[i] - eye(a.shape[1])
        total = jnp.sum(off * off)
        worst = jnp.maximum(worst, jnp.where(total < 1e30, total, 1e30))
    return worst


def factor(a, z, first, start, wide, count, fixed, most):
    for i in range(count):
        first[i] = a[i]
        start[i] = z[i]
    for step in range(fixed):
        for i in range(count):
            newton_step(a.at[i], z.at[i], step < 2)

    def unsettled(state):
        return jnp.logical_and(state[0] < most, state[1] > 3e-5)

    def again(state):
        for i in range(count):
            newton_step(a.at[i], z.at[i])
        return state[0] + 1, residual(a, count)

    left = lax.while_loop(unsettled, again, (jnp.int32(fixed), residual(a, count)))[1]

    @pl.when(left > 3e-5)
    def _():
        def direct(i, _):
            chol_inv(first.at[i], z.at[i], wide)
            z[i] = mm3(z[i], start[i])
            return 0

        lax.fori_loop(0, count, direct, 0)


class Phases:
    def __init__(self, sends, arrivals):
        self.sends, self.arrivals = sends, arrivals
        self.flying = []
        me = lax.axis_index("space")
        self.core = lax.rem(me, 2)
        self.y = lax.rem(me // 2, 4)
        self.x = me // 8
        self.snap = lax.axis_index("snap")
        self.place = lax.rem(self.snap, 4)
        self.used = 0

    def space(self, x, y, core):
        return (x * 4 + y) * 2 + core

    def peers(self):
        found = [{"space": self.space(self.x, self.y, 1 - self.core)}]
        for d in (1, 2, 3):
            found.append({"space": self.space(lax.rem(self.x + d, 4), self.y, self.core)})
            found.append({"space": self.space(self.x, lax.rem(self.y + d, 4), self.core)})
            found.append({"snap": self.other(d)})
        return found

    def other(self, d):
        place = self.place
        if d & 1:
            place = place + 1 - 2 * lax.rem(place, 2)
        if d & 2:
            place = place + 2 - 4 * (place // 2)
        return self.snap - self.place + place

    def send(self, src, dst, device):
        slot = self.used
        self.used += 1
        copy = pltpu.make_async_remote_copy(
            src_ref=src,
            dst_ref=dst,
            send_sem=self.sends.at[slot],
            recv_sem=self.arrivals.at[slot],
            device_id=device,
            device_id_type=MESH,
        )
        copy.start()
        self.flying.append(copy)
        return copy

    def finish(self):
        for copy in self.flying:
            copy.wait_send()

    def greet(self, devices):
        barrier = pltpu.get_barrier_semaphore()
        for device in devices:
            pl.semaphore_signal(barrier, inc=1, device_id=device, device_id_type=MESH)

    def met(self, count):
        pl.semaphore_wait(pltpu.get_barrier_semaphore(), count)

    def along(self, half, major, d):
        if (half == 0) == major:
            place = lax.rem(self.x + d, 4)
            return place, {"space": self.space(place, self.y, self.core)}
        place = lax.rem(self.y + d, 4)
        return place, {"space": self.space(self.x, place, self.core)}

    def own(self, half, major):
        return self.x if (half == 0) == major else self.y


def rows_of(place, size):
    return pl.ds(pl.multiple_of(place * size, size), size)


def sum_over_space(ph, part, bc, bx, by, s1, s2, s3, spread, beside, after):
    twin = {"space": ph.space(ph.x, ph.y, 1 - ph.core)}
    copy = ph.send(part.at[:, :, rows_of(1 - ph.core, 128), :], bc, twin)
    copy.wait_recv()
    s1[...] = part[:, :, rows_of(ph.core, 128), :] + bc[...]
    copies = []
    for d in (1, 2, 3):
        for half in (0, 1):
            place, device = ph.along(half, True, d)
            copies.append(ph.send(s1.at[half, :, rows_of(place, 32), :], bx.at[half, d - 1], device))
    beside()
    for copy in copies:
        copy.wait_recv()
    for half in (0, 1):
        mine = s1[half, :, rows_of(ph.own(half, True), 32), :]
        s2[half] = mine + (bx[half, 0] + bx[half, 1] + bx[half, 2])
    copies = []
    for d in (1, 2, 3):
        for half in (0, 1):
            place, device = ph.along(half, False, d)
            copies.append(ph.send(s2.at[half, :, rows_of(place, 8), :], by.at[half, d - 1], device))
    for copy in copies:
        copy.wait_recv()
    for half in (0, 1):
        mine = s2[half, :, rows_of(ph.own(half, False), 8), :]
        s3[half] = mine + (by[half, 0] + by[half, 1] + by[half, 2])
    copies = []
    for d in (1, 2, 3):
        copies.append(ph.send(s3, spread.at[d], {"snap": ph.other(d)}))
    spread[0] = s3[...]
    for copy in copies:
        copy.wait_recv()
    after()


def give_over_space(ph, chunk, g1, out, beside=None):
    copies = []
    for half in (0, 1):
        mine = rows_of(ph.own(half, False), 8)
        for d in (1, 2, 3):
            _, device = ph.along(half, False, d)
            copies.append(ph.send(chunk.at[half], g1.at[half, :, mine, :], device))
        g1[half, :, mine, :] = chunk[half]
    for copy in copies:
        copy.wait_recv()
    twin = {"space": ph.space(ph.x, ph.y, 1 - ph.core)}
    copies, last = {}, []
    for d in (1, 3, 2):
        for half in (0, 1):
            mine = rows_of(ph.core * 4 + ph.own(half, True), 32)
            _, device = ph.along(half, True, d)
            copies[d, half] = ph.send(g1.at[half], out.at[half, :, mine, :], device)
    for half in (0, 1):
        mine = rows_of(ph.core * 4 + ph.own(half, True), 32)
        last.append(ph.send(g1.at[half], out.at[half, :, mine, :], twin))
        out[half, :, mine, :] = g1[half]
    if beside is not None:
        beside()
    for d in (1, 3, 2):
        for half in (0, 1):
            copies[d, half].wait_recv()
            origin = lax.rem(ph.own(half, True) + 4 - d, 4)
            theirs = out.at[half, :, rows_of(ph.core * 4 + origin, 32), :]
            last.append(ph.send(theirs, theirs, twin))
    for copy in last:
        copy.wait_recv()


def put_halves(ref, index, square):
    ref[0, index] = square[:, :128]
    ref[1, index] = square[:, 128:]


def whole(ref, index):
    return jnp.concatenate([ref[0, index], ref[1, index]], axis=1)


def quarter_rows(place, size):
    return rows_of(2 * lax.rem(place, 2) + place // 2, size)


def first_sum(
    count_ref, x_ref, volume_ref, om_ref, out_ref, parts_ref, zo_ref, weight_ref,
    part, bc, bx, by, s1, s2, s3, spread, chunk, g1, got, sends, arrivals,
    raw, om_local, volume_local, loads, local, parts, m, zo, wide
):
    ph = Phases(sends, arrivals)
    load = pltpu.make_async_copy(x_ref, raw, loads.at[0])
    load.start()
    om_load = pltpu.make_async_copy(om_ref.at[ph.core], om_local, loads.at[1])
    om_load.start()
    volume_load = pltpu.make_async_copy(volume_ref, volume_local, loads.at[2])
    volume_load.start()
    ph.greet(ph.peers())
    used = count_ref[0] * BLOCK
    rows = raw.shape[0]
    total = rows * lax.axis_size("space")
    volume_load.wait()
    volume = volume_local[...].reshape(1, rows)
    weight = jnp.where(iota((1, rows), 1) < used, volume, 0.0) / total
    weight_ref[...] = weight
    load.wait()
    local[...] = jnp.where(iota(raw.shape, 0) < used, raw[...], 0)
    weighted = jnp.transpose(local[...]).astype(F32) * weight
    put_halves(part, 0, mm2(weighted, local[...]))
    ph.met(10)
    quarter = parts.shape[1]

    def give_rows(d):
        there = ph.other(d)
        rows = quarter_rows(lax.rem(there, 4), quarter)
        return ph.send(local.at[rows, :], parts.at[d - 1], {"snap": there})

    bulk = [give_rows(2), give_rows(1)]
    om_load.wait()
    om = om_local[...]
    m[...] = mm(om, om, TN)
    mine = zo.at[ph.core]
    sum_over_space(
        ph, part, bc, bx, by, s1, s2, s3, spread,
        lambda: chol_upper(m, mine, wide),
        lambda: bulk.append(give_rows(3)),
    )
    for d in range(4):
        chunk[:, d] = spread[d, :, 0]
    give_over_space(ph, chunk, g1, got, lambda: chol_lower(mine, wide))
    factor_copy = ph.send(mine, mine, {"space": ph.space(ph.x, ph.y, 1 - ph.core)})
    for d in range(4):
        out_ref[d] = whole(got, d)
    parts_ref[0] = local[quarter_rows(ph.place, quarter), :]
    for d, copy in zip((2, 1, 3), bulk):
        copy.wait_recv()
        parts_ref[d] = parts[d - 1]
    factor_copy.wait_recv()
    zo_ref[...] = zo[...]
    ph.finish()


def gram_factors(g_ref, z, a, first, start, wide):
    rank = g_ref.shape[1]
    diagonal = iota((rank, rank), 0) == iota((rank, rank), 1)
    for d in range(4):
        g = g_ref[d]
        pivots = jnp.where(diagonal, g, 0.0)
        down = lax.rsqrt(jnp.sum(pivots, axis=1, keepdims=True))
        across = lax.rsqrt(jnp.sum(pivots, axis=0, keepdims=True))
        a[d] = g * down * across
        z[d] = jnp.where(diagonal, down, 0.0)
    factor(a, z, first, start, wide, 4, 3, 8)


def second_sum(
    z_ref, x_ref, weight_ref, om_ref, zo_ref, out_ref, sk_ref, q_ref,
    part, bc, bx, by, s1, s2, s3, spread, chunk, g1, got, sends, arrivals, base, sketch
):
    ph = Phases(sends, arrivals)
    ph.greet(ph.peers())
    rank = om_ref.shape[2]
    quarter = x_ref.shape[1]
    for d in range(4):
        base[lax.rem(ph.other(d), 4)] = mm2r(x_ref[d], z_ref[d], NT).astype(BF16)
    weight = weight_ref[:, quarter_rows(ph.place, quarter)]
    mine = sketch.at[2 * lax.rem(ph.place, 2) + ph.place // 2]
    for pair in (0, 1):
        low, high = base[2 * pair], base[2 * pair + 1]
        both = mm(low, om_ref[0, :rank, :]) + mm(high, om_ref[0, rank:, :])
        mine[:, pair * rank : (pair + 1) * rank] = both.astype(BF16)

    pairs = ((base[0], base[1]), (base[2], base[3]), (mine[:, :rank], mine[:, rank:]))
    for index, (low, high) in enumerate(pairs):
        put_halves(part, index, mm2(jnp.transpose(low).astype(F32) * weight, high))
    ph.met(10)
    piece = quarter // 2

    def give_sketch(d, i):
        rows = mine.at[pl.ds(i * piece, piece), :]
        return ph.send(rows, rows, {"snap": ph.other(d)})

    def omega_products():
        for level in (0, 1):
            q_ref[level, 0] = mm2(zo_ref[level], om_ref[level, :rank, :], NT)
            q_ref[level, 1] = mm2r(om_ref[level, rank:, :], zo_ref[level], NT)

    bulk = [give_sketch(2, 0), give_sketch(1, 0)]
    sum_over_space(
        ph, part, bc, bx, by, s1, s2, s3, spread,
        omega_products,
        lambda: bulk.extend([give_sketch(2, 1), give_sketch(1, 1)]),
    )
    chunk[...] = (spread[0] + spread[1]) + (spread[2] + spread[3])
    give_over_space(ph, chunk, g1, got)
    for d in range(3):
        out_ref[d] = whole(got, d)
    for copy in bulk:
        copy.wait_recv()
    for i, d in enumerate((0, 2, 1)):
        there = lax.rem(ph.other(d), 4)
        sk_ref[i] = sketch[2 * lax.rem(there, 2) + there // 2]
    ph.finish()


def sum_scratch(before, after, copies):
    return [
        pltpu.VMEM((2, before, 128, 128), F32),
        pltpu.VMEM((2, 3, before, 32, 128), F32),
        pltpu.VMEM((2, 3, before, 8, 128), F32),
        pltpu.VMEM((2, before, 128, 128), F32),
        pltpu.VMEM((2, before, 32, 128), F32),
        pltpu.VMEM((2, before, 8, 128), F32),
        pltpu.VMEM((4, 2, before, 8, 128), F32),
        pltpu.VMEM((2, after, 8, 128), F32),
        pltpu.VMEM((2, after, 32, 128), F32),
        pltpu.VMEM((2, after, 256, 128), F32),
        pltpu.SemaphoreType.DMA((copies,)),
        pltpu.SemaphoreType.DMA((copies,)),
    ]


def near_identity(qa, cross, qb, a, t):
    t[...] = mm3(qa, mm3(cross, qb))
    a[...] = eye(cross.shape[0]) + t[...] + jnp.transpose(t[...])


def merge_factors(c_ref, zo_ref, q_ref, z, a, first, start, t, wide):
    for pair in (0, 1):
        near_identity(q_ref[0, 0], c_ref[pair], q_ref[0, 1], a.at[pair], t.at[pair])
        z[pair] = zo_ref[0]
    factor(a, z, first, start, wide, 2, 3, 8)
    t[0] = mm3(q_ref[1, 0], z[0])
    t[1] = mm3(jnp.transpose(z[1]), q_ref[1, 1])
    near_identity(t[0], c_ref[2], t[1], a.at[2], t.at[0])
    z[2] = zo_ref[1]
    factor(a.at[pl.ds(2, 1)], z.at[pl.ds(2, 1)], first, start, wide, 1, 3, 8)


def spread_kernel(
    rim_ref, sk_ref, z_ref, om_ref, out_ref, own, base, rim_out, rim_in, sends, arrivals
):
    ph = Phases(sends, arrivals)
    me, n = lax.axis_index("space"), lax.axis_size("space")
    near = ph.other(1)
    before, after = lax.rem(me + n - 1, n), lax.rem(me + 1, n)
    targets = [{"space": before}, {"space": after}]
    targets += [{"space": before, "snap": near}, {"space": after, "snap": near}]
    ph.greet([{"snap": near}] + targets)
    rank = om_ref.shape[2]
    mix = []
    for pair in (0, 1):
        u = mm2r(om_ref[1, pair * rank : (pair + 1) * rank, :], z_ref[2], NT)
        mix.append(mm3(jnp.transpose(z_ref[pair]), u))
    high, low = split(jnp.concatenate(mix, axis=0))
    half = base.shape[0] // 2
    quarter = half // 2
    upper = lax.rem(ph.place, 2)
    second = ph.place // 2

    def rows_from(sk):
        found = (mm(sk, high) + mm(sk, low)).astype(BF16)
        return found.reshape(quarter, *own.shape[1:])

    own[pl.ds((1 - second) * quarter, quarter)] = rows_from(sk_ref[1])
    ph.met(5)
    sent = upper * half + (1 - second) * quarter
    copy = ph.send(
        own.at[pl.ds((1 - second) * quarter, quarter)],
        base.at[pl.ds(sent, quarter)],
        {"snap": near},
    )
    own[pl.ds(second * quarter, quarter)] = rows_from(sk_ref[0])
    for side in (0, 1):
        where = rim_ref[0, side] - upper * half
        block = own[jnp.clip(where, 0, half - 1)]
        inside = jnp.logical_and(where >= 0, where < half)
        rim_out[side] = jnp.where(inside, block, jnp.zeros_like(block))
    swaps = [
        ph.send(rim_out.at[0], rim_in.at[1, 0], targets[0]),
        ph.send(rim_out.at[1], rim_in.at[0, 0], targets[1]),
        ph.send(rim_out.at[0], rim_in.at[1, 1], targets[2]),
        ph.send(rim_out.at[1], rim_in.at[0, 1], targets[3]),
    ]
    base[pl.ds(upper * half, half)] = own[...]
    base[pl.ds((1 - upper) * half + second * quarter, quarter)] = rows_from(sk_ref[2])
    for swap in swaps:
        swap.wait_recv()
    blocks = base.shape[0]
    out_ref[blocks] = jnp.where(me > 0, rim_in[0, 0] + rim_in[0, 1], 0)
    out_ref[blocks + 1] = jnp.where(me < n - 1, rim_in[1, 0] + rim_in[1, 1], 0)
    copy.wait_recv()
    out_ref[:blocks] = base[...]
    ph.finish()


def product_kernel(cols_ref, count_ref, full_ref, jac_ref, base_ref, out_ref, product, sems):
    rank = full_ref.shape[2]
    blocks = jac_ref.shape[0] // BLOCK
    count = count_ref[0]
    copies = [pltpu.make_async_copy(full_ref.at[pl.ds(0, blocks)], base_ref, sems.at[0])]
    copies[0].start()
    pieces = 4
    size = blocks // pieces
    for piece in range(pieces):

        def block(i, _):
            b = piece * size + i
            picked = [full_ref[cols_ref[b, k]] for k in range(NNZ)]
            here = pl.ds(pl.multiple_of(b * BLOCK, BLOCK), BLOCK)
            found = mm(jac_ref[here, :], jnp.concatenate(picked, axis=0))
            product[b] = jnp.where(b < count, found, 0.0).astype(BF16)
            return 0

        lax.fori_loop(0, size, block, 0, unroll=6)
        done = pl.ds(piece * size, size)
        copies.append(
            pltpu.make_async_copy(product.at[done], out_ref.at[done], sems.at[piece + 1])
        )
        copies[-1].start()
    for copy in copies:
        copy.wait()


VM = pl.BlockSpec(memory_space=pltpu.VMEM)
SM = pl.BlockSpec(memory_space=pltpu.SMEM)
HBM = pl.BlockSpec(memory_space=pltpu.HBM)


def call(body, outs, ins, scratch, name, out=VM, limit=VMEM_LIMIT, **params):
    return pl.pallas_call(
        body,
        out_shape=outs,
        in_specs=ins,
        out_specs=jax.tree.map(lambda _: out, outs),
        scratch_shapes=scratch,
        compiler_params=pltpu.CompilerParams(vmem_limit_bytes=limit, **params),
        name=name,
    )


def on_device(snapshots, cell_volume, counts, rim_rows, jac_cols, jacobian, omega):
    rows, rank = snapshots.shape
    blocks, quarter = rows // BLOCK, rows // 4
    square = (rank, rank)
    wide = pltpu.VMEM((rank // 2, rank), F32)

    def squares(n):
        return pltpu.VMEM((n, rank, rank), F32)

    grams, parts, starts, weight = call(
        first_sum,
        [
            jax.ShapeDtypeStruct((4, rank, rank), F32),
            jax.ShapeDtypeStruct((4, quarter, rank), BF16),
            jax.ShapeDtypeStruct((2, rank, rank), F32),
            jax.ShapeDtypeStruct((1, rows), F32),
        ],
        [SM, HBM, HBM, HBM],
        [pltpu.VMEM((2, 1, rank, rank // 2), F32)]
        + sum_scratch(1, 4, 40)
        + [
            pltpu.VMEM((rows, rank), BF16),
            pltpu.VMEM((2 * rank, rank), BF16),
            pltpu.VMEM((rows,), F32),
            pltpu.SemaphoreType.DMA((3,)),
            pltpu.VMEM((rows, rank), BF16),
            pltpu.VMEM((3, quarter, rank), BF16),
            pltpu.VMEM(square, F32),
            squares(2),
            wide,
        ],
        "first_sum",
        limit=60 * 1024 * 1024,
        collective_id=0,
        has_side_effects=True,
    )(counts, snapshots, cell_volume, omega)
    factors = call(
        gram_factors,
        jax.ShapeDtypeStruct((4, rank, rank), F32),
        [VM],
        [squares(4)] * 3 + [wide],
        "gram_factors",
    )(grams)
    cross, sketch, products = call(
        second_sum,
        [
            jax.ShapeDtypeStruct((3, rank, rank), F32),
            jax.ShapeDtypeStruct((3, quarter, 2 * rank), BF16),
            jax.ShapeDtypeStruct((2, 2, rank, rank), F32),
        ],
        [VM] * 5,
        [pltpu.VMEM((2, 3, rank, rank // 2), F32)]
        + sum_scratch(3, 3, 42)
        + [pltpu.VMEM((4, quarter, rank), BF16), pltpu.VMEM((4, quarter, 2 * rank), BF16)],
        "second_sum",
        collective_id=1,
        has_side_effects=True,
    )(factors, parts, weight, omega, starts)
    merged = call(
        merge_factors,
        jax.ShapeDtypeStruct((3, rank, rank), F32),
        [VM] * 3,
        [squares(3), squares(2), squares(2), squares(2), wide],
        "merge_factors",
    )(cross, starts, products)
    full = call(
        spread_kernel,
        jax.ShapeDtypeStruct((blocks + 2, BLOCK, rank), BF16),
        [SM, VM, VM, VM],
        [
            pltpu.VMEM((blocks // 2, BLOCK, rank), BF16),
            pltpu.VMEM((blocks, BLOCK, rank), BF16),
            pltpu.VMEM((2, BLOCK, rank), BF16),
            pltpu.VMEM((2, 2, BLOCK, rank), BF16),
            pltpu.SemaphoreType.DMA((5,)),
            pltpu.SemaphoreType.DMA((5,)),
        ],
        "spread_rows",
        collective_id=2,
        has_side_effects=True,
    )(rim_rows, sketch, merged, omega)
    basis, product = call(
        product_kernel,
        [jax.ShapeDtypeStruct((blocks, BLOCK, rank), BF16)] * 2,
        [SM, SM, VM, VM],
        [pltpu.VMEM((blocks, BLOCK, rank), BF16), pltpu.SemaphoreType.DMA((5,))],
        "jac_product",
        out=HBM,
    )(jac_cols, counts, full, jacobian)
    return (basis.reshape(rows, rank), product.reshape(rows, rank))


def solution(mesh):
    in_specs = (
        P("space", "snap"),
        P("space"),
        P("space"),
        P("space", None),
        P("space", None),
        P("space", None),
        P(),
    )
    out_specs = (P("space", "snap"), P("space", "snap"))
    return jax.shard_map(
        on_device, mesh=mesh, in_specs=in_specs, out_specs=out_specs, check_vma=False
    )
```
